256 devices in a mesh: slab: 4 (over x), xs: 64 (over z, y, core).
Axes of the slice: x: 4, y: 4, z: 8, core: 2. Of those that a mesh axis runs over, the one named last changes fastest.
Arguments:
- perturbation: int32 [4, 1024, 1024], P('slab', 'xs'), may hold values from 0 to 15
- seeds: int32 [4, 32, 2], P('slab'), may hold values from 1 to 8, as said below
Outputs:
- modes: float32 [4, 32, 1024, 1024], P('slab', None, 'xs')
- projected: float32 [4, 32, 32], P('slab')
- correlations: float32 [4, 32, 32], P('slab')
The draws below stay inside these ranges and needn't reach their ends.
Inputs may be any that keep to these rules, and one draw needn't show every extreme that they name: `seeds`: within one slice the 32 pairs (first, second) are distinct; the pairs (1, 1) and (8, 8) occur in every slice.
All inputs are finite; a program needn't handle non-finite values.
Results may differ from the reference program's by a relative error of at most 0.0003.
Values sent between devices are 32-bit elements; how exact they have to be, the bound alone decides.
No kernel may reach another device: no remote copies, remote signals or barrier semaphores. Data moves between devices by JAX's collectives and lax.ppermute only.
A program may use at most 64 MiB of HBM per device.

```python
import math
import jax
import jax.numpy as jnp
from jax import lax

NX = 1024
NY = 1024
M = 32
SWEEPS = 4
KMAX = 8
SLICES = 4


def draw_seeds(key, part):

    def one(slice_key):
        first_key, second_key = jax.random.split(slice_key)
        middle = jax.random.permutation(first_key, KMAX * KMAX - 2) + 1
        picked = jnp.concatenate([jnp.array([0, KMAX * KMAX - 1], dtype=jnp.int32), middle[:M - 2].astype(jnp.int32)])
        picked = jax.random.permutation(second_key, picked)
        first = picked // KMAX + 1
        second = picked % KMAX + 1
        return jnp.stack([first, second], axis=1).astype(jnp.int32)
    keys = jax.random.split(jax.random.fold_in(key, 11), SLICES)
    return jax.vmap(one)(keys)


def place_ends(values, stream_key, low, top_value):
    spot = [jax.random.randint(jax.random.fold_in(stream_key, axis), (), 0, length) for axis, length in enumerate(values.shape)]
    widest = values.shape.index(max(values.shape))
    next_to = spot[:widest] + [(spot[widest] + 1) % values.shape[widest]] + spot[widest + 1:]
    return values.at[tuple(spot)].set(low).at[tuple(next_to)].set(top_value)


def setup_inputs(seed: int = 0) -> dict:
    key_of = jax.random.split(jax.random.key(seed), 3)
    perturbation = place_ends(jax.random.randint(key_of[0], (SLICES, NX, NY), 0, 16), jax.random.fold_in(key_of[0], 1), 0, 15).astype(jnp.int32)
    seeds = draw_seeds(jax.random.fold_in(key_of[2], 71), 0)
    return {"perturbation": perturbation, "seeds": seeds}


def potential(pert, row_ids):
    xpos = (row_ids.astype(jnp.float32)[:, None] + 0.5) / NX - 0.5
    ypos = (jnp.arange(NY).astype(jnp.float32)[None, :] + 0.5) / NY - 0.5
    conf = 4.0 * (xpos * xpos + 0.6 * ypos * ypos + 0.5 * xpos)
    return conf + 0.1 * pert.astype(jnp.float32)

def start_basis(seeds_f, row_ids):
    scale = 2.0 / math.sqrt((NX + 1) * (NY + 1))
    rows_f = row_ids.astype(jnp.float32) + 1.0
    cols_f = jnp.arange(NY).astype(jnp.float32) + 1.0
    along_x = jnp.sin(math.pi * seeds_f[:, 0:1] * rows_f[None, :] / (NX + 1))
    along_y = jnp.sin(math.pi * seeds_f[:, 1:2] * cols_f[None, :] / (NY + 1))
    return scale * along_x[:, :, None] * along_y[:, None, :]

def apply_ham(basis, pot):
    padded = jnp.pad(basis, ((0, 0), (1, 1), (1, 1)))
    beside = padded[:, 2:, 1:-1] + padded[:, :-2, 1:-1] + padded[:, 1:-1, 2:] + padded[:, 1:-1, :-2]
    return 4.0 * basis - beside + pot[None] * basis

def one_slice(inputs):
    pert, seed_pairs = inputs
    row_ids = jnp.arange(NX).astype(jnp.int32)
    pot = potential(pert, row_ids)
    basis = start_basis(seed_pairs.astype(jnp.float32), row_ids)
    for sweep in range(SWEEPS):
        trial = 13.0 * basis - apply_ham(basis, pot)
        gram = jnp.einsum('mij,nij->mn', trial, trial, precision=lax.Precision.HIGHEST)
        lower = jnp.linalg.cholesky(gram)
        identity = jnp.eye(gram.shape[0], dtype=gram.dtype)
        inverse = lax.linalg.triangular_solve(lower, identity, left_side=True, lower=True)
        basis = jnp.einsum('kij,mk->mij', trial, inverse, precision=lax.Precision.HIGHEST)
    image = apply_ham(basis, pot)
    proj = jnp.einsum('mij,nij->mn', basis, image, precision=lax.Precision.HIGHEST)
    return (basis, proj)

def reference(perturbation, seeds):
    bases, projected = lax.map(one_slice, (perturbation, seeds))
    count = bases.shape[0]

    def correlation(index):
        following = jnp.minimum(index + 1, count - 1)
        value = jnp.einsum('mij,nij->mn', bases[index], bases[following], precision=lax.Precision.HIGHEST)
        return jnp.where(index < count - 1, value, jnp.zeros_like(value))
    correlations = lax.map(correlation, jnp.arange(count).astype(jnp.int32))
    modes = bases * math.sqrt(NX * NY)
    return (modes, projected, correlations)
```

```python
import functools
import math

import jax
import jax.numpy as jnp
from jax import lax
from jax.experimental import pallas as pl
from jax.experimental.pallas import tpu as pltpu
from jax.sharding import PartitionSpec as P

NX = 1024
NY = 1024
M = 32
KMAX = 8
ROWS = 16
HALO = 4
EXT = ROWS + 2 * HALO
LANES = 128
TILES = NY // LANES
F32 = jnp.float32
BF16 = jnp.bfloat16


def lane_tile(v):
    return slice(v * LANES, (v + 1) * LANES)


def split(x):
    high = x.astype(BF16)
    return high, (x - high.astype(F32)).astype(BF16)


def dot_t(a, b):
    return lax.dot_general(a, b, (((1,), (1,)), ((), ())), preferred_element_type=F32)


def prepare(k, strip_ref, xtab_ref, ytab_ref, w_ref, sy_ref, sx_ref):
    row = lax.broadcasted_iota(jnp.int32, (EXT, LANES), 0) + (k * ROWS - HALO)
    xpos = (row.astype(F32) + 0.5) / NX - 0.5
    for v in range(TILES):
        col = lax.broadcasted_iota(jnp.int32, (EXT, LANES), 1) + v * LANES
        ypos = (col.astype(F32) + 0.5) / NY - 0.5
        pert = strip_ref[0:EXT, lane_tile(v)].astype(F32)
        pot = 4.0 * (xpos * xpos + 0.6 * ypos * ypos + 0.5 * xpos) + 0.1 * pert
        rest = 9.0 - pot
        for r in range(EXT):
            w_ref[r, :, lane_tile(v)] = jnp.broadcast_to(rest[r : r + 1], (8, LANES))
    seeds = strip_ref[EXT : EXT + 1, 0:LANES].astype(F32)
    spread = jnp.transpose(jnp.broadcast_to(seeds, (LANES, LANES)))
    first, second = spread[0:M], spread[M : 2 * M]
    shift = jnp.zeros((M, LANES), F32)
    along_x = jnp.zeros((M, LANES), F32)
    for a in range(1, KMAX + 1):
        twice = 2.0 * math.cos(math.pi * a / (NX + 1))
        shift += jnp.where(first == a, twice, 0.0) + jnp.where(second == a, twice, 0.0)
        along_x = jnp.where(first == a, xtab_ref[a - 1 : a, :], along_x)
    for r in range(EXT):
        sx_ref[r] = jnp.broadcast_to(along_x[:, r : r + 1], (M, LANES))
    for v in range(TILES):
        along_y = jnp.zeros((M, LANES), F32)
        for b in range(1, KMAX + 1):
            along_y = jnp.where(second == b, ytab_ref[b - 1 : b, lane_tile(v)], along_y)
        sy_ref[:, lane_tile(v)] = along_y
    return shift


def first_sweep(shift, w_ref, sy_ref, sx_ref, out_ref):
    def row(r, carry):
        for t in range(M // 8):
            modes = slice(8 * t, 8 * t + 8)
            sx = sx_ref[r, modes, :]
            for v in range(TILES):
                w = w_ref[r, :, lane_tile(v)]
                out_ref[r, modes, lane_tile(v)] = (w + shift[modes]) * (sx * sy_ref[modes, lane_tile(v)])
        return carry

    lax.fori_loop(0, EXT, row, 0)


def sweep(first_row, last_row, w_ref, in_ref, out_ref):
    lane = lax.broadcasted_iota(jnp.int32, (8, LANES), 1)
    at_left, at_right = lane == 0, lane == LANES - 1
    zero = jnp.zeros((8, LANES), F32)

    def row(r, carry):
        for t in range(M // 8):
            modes = slice(8 * t, 8 * t + 8)
            here = [in_ref[r, modes, lane_tile(v)] for v in range(TILES)]
            fore = [zero] + [pltpu.roll(x, 1, 1) for x in here]
            back = [pltpu.roll(x, LANES - 1, 1) for x in here] + [zero]
            for v in range(TILES):
                left = jnp.where(at_left, fore[v], fore[v + 1])
                right = jnp.where(at_right, back[v + 1], back[v])
                above = in_ref[r - 1, modes, lane_tile(v)]
                below = in_ref[r + 1, modes, lane_tile(v)]
                w = w_ref[r, :, lane_tile(v)]
                out_ref[r, modes, lane_tile(v)] = (w * here[v] + (left + right)) + (above + below)
        return carry

    lax.fori_loop(first_row, last_row + 1, row, 0)


def keep_ends(k, ref):
    ref[HALO - 1] = ref[HALO - 1] * (k > 0).astype(F32)
    ref[EXT - HALO] = ref[EXT - HALO] * (k < NX // ROWS - 1).astype(F32)


def trial(k, margin, strip_ref, xtab_ref, ytab_ref, w_ref, sy_ref, sx_ref, one_ref, two_ref):
    shift = prepare(k, strip_ref, xtab_ref, ytab_ref, w_ref, sy_ref, sx_ref)
    first_sweep(shift, w_ref, sy_ref, sx_ref, one_ref)
    keep_ends(k, one_ref)
    low, high = HALO - margin, EXT - HALO - 1 + margin
    sweep(low - 2, high + 2, w_ref, one_ref, two_ref)
    keep_ends(k, two_ref)
    sweep(low - 1, high + 1, w_ref, two_ref, one_ref)
    keep_ends(k, one_ref)
    sweep(low, high, w_ref, one_ref, two_ref)
    keep_ends(k, two_ref)


def own_kernel(k_ref, strip_ref, xtab_ref, ytab_ref, parts_ref, sums_ref, w_ref, sy_ref, sx_ref, one_ref, two_ref):
    k = k_ref[0]
    trial(k, 1, strip_ref, xtab_ref, ytab_ref, w_ref, sy_ref, sx_ref, one_ref, two_ref)
    sweep(HALO, EXT - HALO - 1, w_ref, two_ref, one_ref)

    def row(r, total):
        high, low = split(two_ref[r + HALO])
        image_high, image_low = split(one_ref[r + HALO])
        parts_ref[r] = jnp.concatenate([high, low, high], axis=0)
        left = jnp.concatenate([high, low], axis=0)
        right = jnp.concatenate([high, image_high, low, image_low], axis=0)
        return total + dot_t(left, right)

    total = lax.fori_loop(0, ROWS, row, jnp.zeros((2 * M, 4 * M), F32))
    total = total[:, 0 : 2 * M] + total[:, 2 * M : 4 * M]
    sums_ref[...] = total[0:M] + total[M : 2 * M]


def next_kernel(k_ref, strip_ref, xtab_ref, ytab_ref, parts_ref, own_ref, sums_ref, w_ref, sy_ref, sx_ref, one_ref, two_ref):
    k = k_ref[0]
    trial(k, 0, strip_ref, xtab_ref, ytab_ref, w_ref, sy_ref, sx_ref, one_ref, two_ref)

    def row(r, total):
        high, low = split(two_ref[r + HALO])
        right = jnp.concatenate([high, low], axis=0)
        left = jnp.concatenate([right, parts_ref[r, 0 : 2 * M, :]], axis=0)
        return total + dot_t(left, right)

    total = lax.fori_loop(0, ROWS, row, jnp.zeros((4 * M, 2 * M), F32))
    total = total[:, 0:M] + total[:, M : 2 * M]
    gram, across = total[0:M] + total[M : 2 * M], total[2 * M : 3 * M] + total[3 * M : 4 * M]
    sums_ref[...] = jnp.concatenate([own_ref[...], gram, across], axis=1)


def finish_kernel(keep_ref, sums_ref, parts_ref, modes_ref, proj_ref, corr_ref, held_ref, sem):
    sums = sums_ref[...]
    row = lax.broadcasted_iota(jnp.int32, (M, LANES), 0)
    lane = lax.broadcasted_iota(jnp.int32, (M, LANES), 1)
    is_gram = (lane // M) % 2 == 0
    work = jnp.where(is_gram, sums, (lane % M == row).astype(F32))
    pivots = jnp.ones((M, LANES), F32)
    for j in range(M):
        column = jnp.where(lane < 2 * M, work[:, j : j + 1], work[:, 2 * M + j : 2 * M + j + 1])
        pivots = jnp.where(row == j, column, pivots)
        scaled = work[j : j + 1, :] / column[j : j + 1, :]
        work = work - jnp.where(row > j, column, 0.0) * scaled
    inverse = work / jnp.sqrt(pivots)
    own, following = inverse[:, M : 2 * M], inverse[:, 3 * M : 4 * M]
    high, low = split(own * math.sqrt(NX * NY))
    factors = jnp.concatenate([high, high, low], axis=1)

    copies = []
    width = NY // 4
    for c in range(4):
        cols = slice(c * width, (c + 1) * width)
        for r in range(ROWS):
            held_ref[:, r, cols] = jnp.dot(factors, parts_ref[r, :, cols], preferred_element_type=F32)
        copy = pltpu.make_async_copy(held_ref.at[:, :, cols], modes_ref.at[:, :, cols], sem.at[c])
        copy.start()
        copies.append(copy)

    exact = functools.partial(jnp.dot, precision=lax.Precision.HIGHEST, preferred_element_type=F32)
    image, across = sums[:, M : 2 * M], sums[:, 3 * M : 4 * M]
    eye = (row == lane)[:, 0:M].astype(F32)
    proj_ref[...] = 13.0 * eye - exact(exact(own, image), own.T)
    corr_ref[...] = jnp.where(keep_ref[0] > 0, exact(exact(own, across), following.T), 0.0)
    for copy in copies:
        copy.wait()


def add_over_strips(v):
    def others(x, *masks):
        return [lax.ppermute(x, "xs", [(i, i ^ mask) for i in range(64)]) for mask in masks]

    v = v + others(v, 1)[0]
    for unit in (2, 8):
        one, two, three = others(v, unit, 2 * unit, 3 * unit)
        v = (v + one) + (two + three)
    return v + others(v, 7 * 8)[0]


def local(perturbation, seeds):
    k = lax.axis_index("xs")
    slab = lax.axis_index("slab")
    strips = NX // ROWS
    pert = perturbation[0]
    before = lax.ppermute(pert[ROWS - HALO :], "xs", [(i, i + 1) for i in range(strips - 1)])
    after = lax.ppermute(pert[:HALO], "xs", [(i + 1, i) for i in range(strips - 1)])
    flat = jnp.pad(seeds[0].T.reshape(1, 2 * M), ((0, 7), (0, NY - 2 * M)))
    strip = jnp.concatenate([before, pert, after, flat], axis=0)
    following = lax.ppermute(strip, "slab", [((i + 1) % 4, i) for i in range(4)])

    index = jnp.arange(1, KMAX + 1).astype(F32)[:, None]
    rows = (k * ROWS - HALO + jnp.arange(LANES)).astype(F32)[None, :] + 1.0
    cols = jnp.arange(NY).astype(F32)[None, :] + 1.0
    scale = 2.0 / math.sqrt((NX + 1) * (NY + 1))
    xtab = scale * jnp.sin(math.pi * index * rows / (NX + 1))
    ytab = jnp.sin(math.pi * index * cols / (NY + 1))
    kk = k.reshape(1).astype(jnp.int32)

    smem = pl.BlockSpec(memory_space=pltpu.SMEM)
    vmem = pl.BlockSpec(memory_space=pltpu.VMEM)
    scratch = [
        pltpu.VMEM((EXT, 8, NY), F32),
        pltpu.VMEM((M, NY), F32),
        pltpu.VMEM((EXT, M, LANES), F32),
        pltpu.VMEM((EXT, M, NY), F32),
        pltpu.VMEM((EXT, M, NY), F32),
    ]
    parts, own = pl.pallas_call(
        own_kernel,
        name="own_trial",
        out_shape=(jax.ShapeDtypeStruct((ROWS, 3 * M, NY), BF16), jax.ShapeDtypeStruct((M, 2 * M), F32)),
        in_specs=[smem, vmem, vmem, vmem],
        out_specs=(vmem, vmem),
        scratch_shapes=scratch,
        compiler_params=pltpu.CompilerParams(vmem_limit_bytes=24 * 2**20),
        cost_estimate=pl.CostEstimate(flops=2 * 2**28, bytes_accessed=2**23, transcendentals=0),
    )(kk, strip, xtab, ytab)
    sums = pl.pallas_call(
        next_kernel,
        name="next_trial",
        out_shape=jax.ShapeDtypeStruct((M, 4 * M), F32),
        in_specs=[smem, vmem, vmem, vmem, vmem, vmem],
        out_specs=vmem,
        scratch_shapes=scratch,
        compiler_params=pltpu.CompilerParams(vmem_limit_bytes=24 * 2**20),
        cost_estimate=pl.CostEstimate(flops=2 * 2**28, bytes_accessed=2**23, transcendentals=0),
    )(kk, following, xtab, ytab, parts, own)
    sums = add_over_strips(sums)
    keep = (slab < 3).reshape(1).astype(jnp.int32)
    modes, projected, correlations = pl.pallas_call(
        finish_kernel,
        name="finish",
        out_shape=(
            jax.ShapeDtypeStruct((M, ROWS, NY), F32),
            jax.ShapeDtypeStruct((M, M), F32),
            jax.ShapeDtypeStruct((M, M), F32),
        ),
        in_specs=[smem, vmem, vmem],
        out_specs=(pl.BlockSpec(memory_space=pl.ANY), vmem, vmem),
        scratch_shapes=[pltpu.VMEM((M, ROWS, NY), F32), pltpu.SemaphoreType.DMA((4,))],
        compiler_params=pltpu.CompilerParams(vmem_limit_bytes=24 * 2**20),
        cost_estimate=pl.CostEstimate(flops=2 * 2**26, bytes_accessed=2**23, transcendentals=0),
    )(keep, sums, parts)
    return modes[None], projected[None], correlations[None]


def solution(mesh):
    return jax.shard_map(
        local,
        mesh=mesh,
        in_specs=(P("slab", "xs", None), P("slab", None, None)),
        out_specs=(P("slab", None, "xs", None), P("slab", None, None), P("slab", None, None)),
        check_vma=False,
    )
```

```python
import functools
import math

import jax
import jax.numpy as jnp
from jax import lax
from jax.experimental import pallas as pl
from jax.experimental.pallas import tpu as pltpu
from jax.sharding import PartitionSpec as P

NX = 1024
NY = 1024
M = 32
ROWS = 16
HALO = 4
EXT = ROWS + 2 * HALO
LANES = 128
GROUPS = LANES // M
SPAN = NY // GROUPS
STEPS = SPAN // 8
F32 = jnp.float32
BF16 = jnp.bfloat16


def split(x):
    high = x.astype(BF16)
    return high, (x - high.astype(F32)).astype(BF16)


def iota(shape, axis):
    return lax.broadcasted_iota(jnp.int32, shape, axis)


def assemble_kernel(k_ref, inner_ref, outer_ref, pert_ref, seeds_ref, strip_ref):
    even = k_ref[0] % 2 == 0
    before = jnp.where(even, outer_ref[ROWS - HALO :, :], inner_ref[ROWS - HALO :, :])
    after = jnp.where(even, inner_ref[:HALO, :], outer_ref[:HALO, :])
    strip_ref[0:HALO, :] = before
    strip_ref[HALO : HALO + ROWS, :] = pert_ref[...]
    strip_ref[HALO + ROWS : EXT, :] = after
    strip_ref[EXT : EXT + 2, 0:LANES] = jnp.concatenate([seeds_ref[...]] * GROUPS, axis=1)


def first_trial(k, strip_ref, w_ref, pert_ref, out_ref):
    unit = math.pi / (NX + 1)
    first = strip_ref[EXT : EXT + 1, 0:LANES].astype(F32)
    second = strip_ref[EXT + 1 : EXT + 2, 0:LANES].astype(F32)
    shift = 2.0 * jnp.cos(unit * first) + 2.0 * jnp.cos(unit * second)

    group, s = iota((8, LANES), 1) // M, iota((8, LANES), 0)
    base = (group * SPAN + s * STEPS).astype(F32)
    scale = 2.0 / math.sqrt((NX + 1) * (NY + 1))
    angle = unit * second * (base + 1.0)
    sin_base, cos_base = scale * jnp.sin(angle), scale * jnp.cos(angle)
    step = unit * second * iota((STEPS, LANES), 0).astype(F32)
    sin_step, cos_step = jnp.sin(step), jnp.cos(step)
    row = iota((EXT, LANES), 0) + (k * ROWS - HALO)
    along_x = jnp.sin(unit * first * (row.astype(F32) + 1.0))
    along_x = jnp.where((row >= 0) & (row < NX), along_x, 0.0)
    xpos = (row.astype(F32) + 0.5) / NX - 0.5
    x_part = 9.0 - 4.0 * (xpos * xpos + 0.5 * xpos)

    pert = strip_ref[0:EXT, :].astype(F32)
    stacked = [pert[:, g * SPAN : (g + 1) * SPAN] for g in range(GROUPS)]
    stacked = jnp.concatenate(stacked + [jnp.zeros((LANES - GROUPS * EXT, SPAN), F32)], axis=0)
    pert_ref[...] = jnp.transpose(stacked)
    spread = jnp.concatenate([pert_ref[pl.ds(q, 8, stride=STEPS), :] for q in range(STEPS)], axis=0).astype(BF16)
    source = iota((LANES, LANES), 0) - EXT * (iota((LANES, LANES), 1) // M)

    sines, y_parts = [], []
    for q in range(STEPS):
        sines.append(sin_base * cos_step[q : q + 1] + cos_base * sin_step[q : q + 1])
        ypos = (base + (q + 0.5)) / NY - 0.5
        y_parts.append(2.4 * ypos * ypos)
    for r in range(EXT):
        here = jnp.dot(spread, (source == r).astype(BF16), preferred_element_type=F32)
        x_row = jnp.broadcast_to(x_part[r : r + 1], (8, LANES))
        sine_row = jnp.broadcast_to(along_x[r : r + 1], (8, LANES))
        for q in range(STEPS):
            w = (x_row - y_parts[q]) - 0.1 * here[8 * q : 8 * q + 8]
            w_ref[r, q] = w
            out_ref[r, q] = (w + shift) * (sine_row * sines[q])


def beyond(row_first, row_last):
    s, lane = iota((8, LANES), 0), iota((8, LANES), 1)
    down = pltpu.roll(row_last, 1, 0)
    left = jnp.where(s == 0, jnp.where(lane < M, 0.0, pltpu.roll(down, M, 1)), down)
    up = pltpu.roll(row_first, 7, 0)
    right = jnp.where(s == 7, jnp.where(lane >= LANES - M, 0.0, pltpu.roll(up, LANES - M, 1)), up)
    return left, right


def sweep(k, first_row, count, in_ref, w_ref, out_ref, shifted=0, hamiltonian=False):
    batch, chunk = count // 2, 4

    def rows(i, carry):
        r = first_row + i * batch
        ends = [beyond(in_ref[r + j, 0], in_ref[r + j, STEPS - 1]) for j in range(batch)]
        factor = {}
        top, bottom = HALO - 1 - first_row, EXT - HALO - first_row - batch
        if 0 <= top < batch:
            factor[top] = jnp.where((i == 0) & (k == 0), 0.0, 1.0)
        if 0 <= bottom < batch:
            factor[bottom] = jnp.where((i == 1) & (k == NX // ROWS - 1), 0.0, 1.0) * factor.get(bottom, 1.0)
        for q0 in range(0, STEPS, chunk):
            inside = range(q0, q0 + chunk)
            x = {(j, q): in_ref[r + j, q] for j in range(-1, batch + 1) for q in inside}
            for j in range(batch):
                x[j, q0 - 1] = in_ref[r + j, q0 - 1] if q0 > 0 else ends[j][0]
                x[j, q0 + chunk] = in_ref[r + j, q0 + chunk] if q0 + chunk < STEPS else ends[j][1]
            for j in range(batch):
                for q in inside:
                    near = (x[j, q - 1] + x[j, q + 1]) + (x[j - 1, q] + x[j + 1, q])
                    if hamiltonian:
                        value = (13.0 - w_ref[r + j, q]) * x[j, q] - near
                    else:
                        value = w_ref[r + j, q] * x[j, q] + near
                    if j in factor:
                        value = value * factor[j]
                    out_ref[r + j - shifted, q] = value
        return carry

    lax.fori_loop(0, 2, rows, 0)


def blocks(product):
    return sum(product[M * g : M * g + M, M * g : M * g + M] for g in range(GROUPS))


def dot_cells(a, b):
    return lax.dot_general(a, b, (((0,), (0,)), ((), ())), preferred_element_type=F32)


def own_kernel(k_ref, strip_ref, modes_ref, sums_ref, w_ref, pert_ref, one_ref, two_ref):
    k = k_ref[0]
    first_trial(k, strip_ref, w_ref, pert_ref, one_ref)
    sweep(k, 1, EXT - 2, one_ref, w_ref, two_ref)
    sweep(k, 2, EXT - 4, two_ref, w_ref, one_ref)
    sweep(k, 3, EXT - 6, one_ref, w_ref, two_ref)
    sweep(k, 4, ROWS, two_ref, w_ref, one_ref, hamiltonian=True)
    field = two_ref[HALO : HALO + ROWS].reshape(ROWS * SPAN, LANES)
    image = one_ref[HALO : HALO + ROWS].reshape(ROWS * SPAN, LANES)
    modes_ref[...] = field
    high, low = split(field)
    image_high, image_low = split(image)
    main = dot_cells(high, jnp.concatenate([high, low, image_high, image_low], axis=1))
    rest = blocks(dot_cells(low, image_high))
    cross = blocks(main[:, LANES : 2 * LANES])
    gram = blocks(main[:, 0:LANES]) + (cross + cross.T)
    ham = blocks(main[:, 2 * LANES : 3 * LANES]) + (blocks(main[:, 3 * LANES :]) + rest)
    sums_ref[...] = jnp.concatenate([gram, ham], axis=1)


def next_kernel(k_ref, strip_ref, modes_ref, own_ref, sums_ref, w_ref, pert_ref, one_ref, two_ref):
    k = k_ref[0]
    first_trial(k, strip_ref, w_ref, pert_ref, one_ref)
    sweep(k, 2, EXT - 4, one_ref, w_ref, two_ref)
    sweep(k, 3, EXT - 6, two_ref, w_ref, one_ref)
    sweep(k, 4, ROWS, one_ref, w_ref, two_ref)
    field = two_ref[HALO : HALO + ROWS].reshape(ROWS * SPAN, LANES)
    high, low = split(field)
    own_high, own_low = split(modes_ref[...])
    main = dot_cells(jnp.concatenate([high, own_high], axis=1), jnp.concatenate([high, low], axis=1))
    rest = blocks(dot_cells(own_low, high))
    cross = blocks(main[0:LANES, LANES:])
    gram = blocks(main[0:LANES, 0:LANES]) + (cross + cross.T)
    across = blocks(main[LANES:, 0:LANES]) + (blocks(main[LANES:, LANES:]) + rest)
    sums_ref[...] = jnp.concatenate([own_ref[...], gram, across], axis=1)


def parts_kernel(modes_ref, parts_ref):
    def rows(i, carry):
        for j in range(4):
            r = i * 4 + j
            pieces = [
                modes_ref[pl.ds(r * SPAN + q * 8 + s, 8, stride=8), :] for s in range(8) for q in range(0, STEPS, 8)
            ]
            parts_ref[r] = jnp.concatenate(split(jnp.concatenate(pieces, axis=0)), axis=1)
        return carry

    lax.fori_loop(0, ROWS // 4, rows, 0)


def finish_kernel(keep_ref, sums_ref, parts_ref, modes_ref, proj_ref, corr_ref, held_ref, sem):
    sums = sums_ref[...]
    row, lane = iota((M, LANES), 0), iota((M, LANES), 1)
    work = jnp.where((lane // M) % 2 == 0, sums, (lane % M == row).astype(F32))
    pivots = jnp.ones((M, LANES), F32)
    for j in range(M):
        column = jnp.where(lane < 2 * M, work[:, j : j + 1], work[:, 2 * M + j : 2 * M + j + 1])
        pivots = jnp.where(row == j, column, pivots)
        scaled = work[j : j + 1, :] / column[j : j + 1, :]
        work = work - jnp.where(row > j, column, 0.0) * scaled
    inverse = work / jnp.sqrt(pivots)
    own, following = inverse[:, M : 2 * M], inverse[:, 3 * M : 4 * M]
    wide = jnp.concatenate([own * math.sqrt(NX * NY)] * GROUPS, axis=1)
    wide = jnp.concatenate([jnp.where(lane // M == g, wide, 0.0) for g in range(GROUPS)], axis=0)
    high, low = split(wide)
    twice = jnp.concatenate([high, high], axis=1)

    def times(a, b):
        return lax.dot_general(a, b, (((1,), (1,)), ((), ())), preferred_element_type=F32)

    copies = []
    for half in range(2):
        for r in range(8 * half, 8 * half + 8):
            part = parts_ref[r]
            result = times(twice, part) + times(low, part[:, 0:LANES])
            for g in range(GROUPS):
                held_ref[:, r, g * SPAN : (g + 1) * SPAN] = result[M * g : M * g + M]
        rows = slice(8 * half, 8 * half + 8)
        copy = pltpu.make_async_copy(held_ref.at[:, rows], modes_ref.at[:, rows], sem.at[half])
        copy.start()
        copies.append(copy)

    exact = functools.partial(jnp.dot, precision=lax.Precision.HIGHEST, preferred_element_type=F32)
    image, across = sums[:, M : 2 * M], sums[:, 3 * M : 4 * M]
    proj_ref[...] = exact(exact(own, image), own.T)
    corr_ref[...] = jnp.where(keep_ref[0] > 0, exact(exact(own, across), following.T), 0.0)
    for copy in copies:
        copy.wait()


def add_over_strips(v):
    def others(x, *masks):
        return [lax.ppermute(x, "xs", [(i, i ^ mask) for i in range(64)]) for mask in masks]

    v = v + others(v, 1)[0]
    for unit in (2, 8):
        one, two, three = others(v, unit, 2 * unit, 3 * unit)
        v = (v + one) + (two + three)
    return v + others(v, 7 * 8)[0]


def local(perturbation, seeds):
    k = lax.axis_index("xs")
    strips = NX // ROWS
    pert = perturbation[0]
    inner = lax.ppermute(pert, "xs", [(i, i ^ 1) for i in range(strips)])
    outer = lax.ppermute(pert, "xs", [(i, i - 1 if i % 2 == 0 else i + 1) for i in range(1, strips - 1)])
    kk = k.reshape(1).astype(jnp.int32)
    keep = (lax.axis_index("slab") < 3).reshape(1).astype(jnp.int32)

    smem = pl.BlockSpec(memory_space=pltpu.SMEM)
    vmem = pl.BlockSpec(memory_space=pltpu.VMEM)
    params = pltpu.CompilerParams(vmem_limit_bytes=28 * 2**20)
    strip = pl.pallas_call(
        assemble_kernel,
        name="assemble",
        out_shape=jax.ShapeDtypeStruct((32, NY), jnp.int32),
        in_specs=[smem, vmem, vmem, vmem, vmem],
        out_specs=vmem,
        compiler_params=pltpu.CompilerParams(vmem_limit_bytes=4 * 2**20),
    )(kk, inner, outer, pert, seeds[0].T)
    following = lax.ppermute(strip, "slab", [((i + 1) % 4, i) for i in range(4)])

    scratch = [
        pltpu.VMEM((EXT, STEPS, 8, LANES), F32),
        pltpu.VMEM((SPAN, LANES), F32),
        pltpu.VMEM((EXT, STEPS, 8, LANES), F32),
        pltpu.VMEM((EXT, STEPS, 8, LANES), F32),
    ]
    cost = pl.CostEstimate(flops=2**30, bytes_accessed=2**23, transcendentals=0)
    field, own = pl.pallas_call(
        own_kernel,
        name="own_trial",
        out_shape=(jax.ShapeDtypeStruct((ROWS * SPAN, LANES), F32), jax.ShapeDtypeStruct((M, 2 * M), F32)),
        in_specs=[smem, vmem],
        out_specs=(vmem, vmem),
        scratch_shapes=scratch,
        compiler_params=params,
        cost_estimate=cost,
    )(kk, strip)
    sums = pl.pallas_call(
        next_kernel,
        name="next_trial",
        out_shape=jax.ShapeDtypeStruct((M, 4 * M), F32),
        in_specs=[smem, vmem, vmem, vmem],
        out_specs=vmem,
        scratch_shapes=scratch,
        compiler_params=params,
        cost_estimate=cost,
    )(kk, following, field, own)
    parts = pl.pallas_call(
        parts_kernel,
        name="parts",
        out_shape=jax.ShapeDtypeStruct((ROWS, SPAN, 2 * LANES), BF16),
        in_specs=[vmem],
        out_specs=vmem,
        compiler_params=pltpu.CompilerParams(vmem_limit_bytes=12 * 2**20),
        cost_estimate=pl.CostEstimate(flops=2**20, bytes_accessed=2**22, transcendentals=0),
    )(field)
    sums = add_over_strips(sums)
    modes, projected, correlations = pl.pallas_call(
        finish_kernel,
        name="finish",
        out_shape=(
            jax.ShapeDtypeStruct((M, ROWS, NY), F32),
            jax.ShapeDtypeStruct((M, M), F32),
            jax.ShapeDtypeStruct((M, M), F32),
        ),
        in_specs=[smem, vmem, vmem],
        out_specs=(pl.BlockSpec(memory_space=pl.ANY), vmem, vmem),
        scratch_shapes=[pltpu.VMEM((M, ROWS, NY), F32), pltpu.SemaphoreType.DMA((2,))],
        compiler_params=params,
        cost_estimate=pl.CostEstimate(flops=2**28, bytes_accessed=2**23, transcendentals=0),
    )(keep, sums, parts)
    return modes[None], projected[None], correlations[None]


def solution(mesh):
    return jax.shard_map(
        local,
        mesh=mesh,
        in_specs=(P("slab", "xs", None), P("slab", None, None)),
        out_specs=(P("slab", None, "xs", None), P("slab", None, None), P("slab", None, None)),
        check_vma=False,
    )
```

```python
import functools
import math

import jax
import jax.numpy as jnp
from jax import lax
from jax.experimental import pallas as pl
from jax.experimental.pallas import tpu as pltpu
from jax.sharding import PartitionSpec as P

NX = 1024
NY = 1024
M = 32
ROWS = 16
HALO = 4
EXT = ROWS + 2 * HALO
LANES = 128
GROUPS = LANES // M
SPAN = NY // GROUPS
STEPS = SPAN // 8
F32 = jnp.float32
BF16 = jnp.bfloat16


def split(x):
    high = x.astype(BF16)
    return high, (x - high.astype(F32)).astype(BF16)


def iota(shape, axis):
    return lax.broadcasted_iota(jnp.int32, shape, axis)


def assemble_kernel(inner_ref, outer_ref, pert_ref, seeds_ref, strip_ref):
    even = lax.axis_index("xs") % 2 == 0
    before = jnp.where(even, outer_ref[ROWS - HALO :, :], inner_ref[ROWS - HALO :, :])
    after = jnp.where(even, inner_ref[:HALO, :], outer_ref[:HALO, :])
    strip_ref[0:HALO, :] = before
    strip_ref[HALO : HALO + ROWS, :] = pert_ref[...]
    strip_ref[HALO + ROWS : EXT, :] = after
    strip_ref[EXT : EXT + 2, 0:LANES] = jnp.concatenate([seeds_ref[...]] * GROUPS, axis=1)


def first_trial(k, strip_ref, w_ref, pert_ref, out_ref):
    unit = math.pi / (NX + 1)
    first = strip_ref[EXT : EXT + 1, 0:LANES].astype(F32)
    second = strip_ref[EXT + 1 : EXT + 2, 0:LANES].astype(F32)
    shift = 2.0 * jnp.cos(unit * first) + 2.0 * jnp.cos(unit * second)

    group, s = iota((8, LANES), 1) // M, iota((8, LANES), 0)
    base = (group * SPAN + s * STEPS).astype(F32)
    scale = 2.0 / math.sqrt((NX + 1) * (NY + 1))
    angle = unit * second * (base + 1.0)
    sin_base, cos_base = scale * jnp.sin(angle), scale * jnp.cos(angle)
    step = unit * second * iota((STEPS, LANES), 0).astype(F32)
    sin_step, cos_step = jnp.sin(step), jnp.cos(step)
    row = iota((EXT, LANES), 0) + (k * ROWS - HALO)
    along_x = jnp.sin(unit * first * (row.astype(F32) + 1.0))
    along_x = jnp.where((row >= 0) & (row < NX), along_x, 0.0)
    xpos = (row.astype(F32) + 0.5) / NX - 0.5
    x_part = 9.0 - 4.0 * (xpos * xpos + 0.5 * xpos)

    pert = strip_ref[0:EXT, :].astype(F32)
    stacked = [pert[:, g * SPAN : (g + 1) * SPAN] for g in range(GROUPS)]
    stacked = jnp.concatenate(stacked + [jnp.zeros((LANES - GROUPS * EXT, SPAN), F32)], axis=0)
    pert_ref[...] = jnp.transpose(stacked)
    spread = jnp.concatenate([pert_ref[pl.ds(q, 8, stride=STEPS), :] for q in range(STEPS)], axis=0).astype(BF16)
    source = iota((LANES, LANES), 0) - EXT * (iota((LANES, LANES), 1) // M)

    sines, y_parts = [], []
    for q in range(STEPS):
        sines.append(sin_base * cos_step[q : q + 1] + cos_base * sin_step[q : q + 1])
        ypos = (base + (q + 0.5)) / NY - 0.5
        y_parts.append(2.4 * ypos * ypos)
    for r in range(EXT):
        here = jnp.dot(spread, (source == r).astype(BF16), preferred_element_type=F32)
        x_row = jnp.broadcast_to(x_part[r : r + 1], (8, LANES))
        sine_row = jnp.broadcast_to(along_x[r : r + 1], (8, LANES))
        for q in range(STEPS):
            w = (x_row - y_parts[q]) - 0.1 * here[8 * q : 8 * q + 8]
            w_ref[r, q] = w
            out_ref[r, q] = (w + shift) * (sine_row * sines[q])


def beyond(row_first, row_last):
    s, lane = iota((8, LANES), 0), iota((8, LANES), 1)
    down = pltpu.roll(row_last, 1, 0)
    left = jnp.where(s == 0, jnp.where(lane < M, 0.0, pltpu.roll(down, M, 1)), down)
    up = pltpu.roll(row_first, 7, 0)
    right = jnp.where(s == 7, jnp.where(lane >= LANES - M, 0.0, pltpu.roll(up, LANES - M, 1)), up)
    return left, right


def sweep(k, first_row, count, in_ref, w_ref, out_ref, shifted=0, hamiltonian=False):
    batch, chunk = count // 2, 4

    def rows(i, carry):
        r = first_row + i * batch
        ends = [beyond(in_ref[r + j, 0], in_ref[r + j, STEPS - 1]) for j in range(batch)]
        factor = {}
        top, bottom = HALO - 1 - first_row, EXT - HALO - first_row - batch
        if 0 <= top < batch:
            factor[top] = jnp.where((i == 0) & (k == 0), 0.0, 1.0)
        if 0 <= bottom < batch:
            factor[bottom] = jnp.where((i == 1) & (k == NX // ROWS - 1), 0.0, 1.0) * factor.get(bottom, 1.0)
        for q0 in range(0, STEPS, chunk):
            inside = range(q0, q0 + chunk)
            x = {(j, q): in_ref[r + j, q] for j in range(-1, batch + 1) for q in inside}
            for j in range(batch):
                x[j, q0 - 1] = in_ref[r + j, q0 - 1] if q0 > 0 else ends[j][0]
                x[j, q0 + chunk] = in_ref[r + j, q0 + chunk] if q0 + chunk < STEPS else ends[j][1]
            for j in range(batch):
                for q in inside:
                    near = (x[j, q - 1] + x[j, q + 1]) + (x[j - 1, q] + x[j + 1, q])
                    if hamiltonian:
                        value = (13.0 - w_ref[r + j, q]) * x[j, q] - near
                    else:
                        value = w_ref[r + j, q] * x[j, q] + near
                    if j in factor:
                        value = value * factor[j]
                    out_ref[r + j - shifted, q] = value
        return carry

    lax.fori_loop(0, 2, rows, 0)


def blocks(product):
    return sum(product[M * g : M * g + M, M * g : M * g + M] for g in range(GROUPS))


def dot_cells(a, b):
    return lax.dot_general(a, b, (((0,), (0,)), ((), ())), preferred_element_type=F32)


def own_kernel(strip_ref, modes_ref, sums_ref, w_ref, pert_ref, one_ref, two_ref):
    k = lax.axis_index("xs")
    first_trial(k, strip_ref, w_ref, pert_ref, one_ref)
    sweep(k, 1, EXT - 2, one_ref, w_ref, two_ref)
    sweep(k, 2, EXT - 4, two_ref, w_ref, one_ref)
    sweep(k, 3, EXT - 6, one_ref, w_ref, two_ref)
    sweep(k, 4, ROWS, two_ref, w_ref, one_ref, hamiltonian=True)
    field = two_ref[HALO : HALO + ROWS].reshape(ROWS * SPAN, LANES)
    image = one_ref[HALO : HALO + ROWS].reshape(ROWS * SPAN, LANES)
    modes_ref[...] = field
    high, low = split(field)
    image_high, image_low = split(image)
    main = dot_cells(high, jnp.concatenate([high, low, image_high, image_low], axis=1))
    rest = blocks(dot_cells(low, image_high))
    cross = blocks(main[:, LANES : 2 * LANES])
    gram = blocks(main[:, 0:LANES]) + (cross + cross.T)
    ham = blocks(main[:, 2 * LANES : 3 * LANES]) + (blocks(main[:, 3 * LANES :]) + rest)
    sums_ref[...] = jnp.concatenate([gram, ham], axis=1)


def next_kernel(strip_ref, modes_ref, own_ref, sums_ref, w_ref, pert_ref, one_ref, two_ref):
    k = lax.axis_index("xs")
    first_trial(k, strip_ref, w_ref, pert_ref, one_ref)
    sweep(k, 2, EXT - 4, one_ref, w_ref, two_ref)
    sweep(k, 3, EXT - 6, two_ref, w_ref, one_ref)
    sweep(k, 4, ROWS, one_ref, w_ref, two_ref)
    field = two_ref[HALO : HALO + ROWS].reshape(ROWS * SPAN, LANES)
    high, low = split(field)
    own_high, own_low = split(modes_ref[...])
    main = dot_cells(jnp.concatenate([high, own_high], axis=1), jnp.concatenate([high, low], axis=1))
    rest = blocks(dot_cells(own_low, high))
    cross = blocks(main[0:LANES, LANES:])
    gram = blocks(main[0:LANES, 0:LANES]) + (cross + cross.T)
    across = blocks(main[LANES:, 0:LANES]) + (blocks(main[LANES:, LANES:]) + rest)
    sums_ref[...] = jnp.concatenate([own_ref[...], gram, across], axis=1)


def parts_kernel(modes_ref, parts_ref):
    def rows(i, carry):
        for j in range(4):
            r = i * 4 + j
            pieces = [
                modes_ref[pl.ds(r * SPAN + q * 8 + s, 8, stride=8), :] for s in range(8) for q in range(0, STEPS, 8)
            ]
            parts_ref[r] = jnp.concatenate(split(jnp.concatenate(pieces, axis=0)), axis=1)
        return carry

    lax.fori_loop(0, ROWS // 4, rows, 0)


def inverse_factors(sums):
    row, lane = iota((8, LANES), 0), iota((8, LANES), 1)
    start = lane // (2 * M) * (2 * M)
    tiles = [
        jnp.where((lane // M) % 2 == 0, sums[8 * t : 8 * t + 8], (lane % M == row + 8 * t).astype(F32))
        for t in range(M // 8)
    ]
    for t in range(M // 8):
        lanes = [start + (8 * t + i) for i in range(8)]
        below = range(t + 1, M // 8)
        columns = [[jnp.take_along_axis(tiles[u], lanes[i], axis=1) for u in below] for i in range(8)]
        rows = [jnp.broadcast_to(tiles[t][i : i + 1], (8, LANES)) for i in range(8)]
        corner = {(i, j): jnp.take_along_axis(rows[i], lanes[j], axis=1) for i in range(8) for j in range(i, 8)}
        inverse, factor = [], {}
        for i in range(8):
            inverse.append(1.0 / corner[i, i])
            for j in range(i + 1, 8):
                factor[j, i] = corner[i, j] * inverse[i]
            for j in range(i + 1, 8):
                for m in range(j, 8):
                    corner[j, m] = corner[j, m] - factor[j, i] * corner[i, m]
        for i in range(8):
            for j in range(i):
                rows[i] = rows[i] - factor[i, j] * rows[j]
                columns[i] = [c - factor[i, j] * p for c, p in zip(columns[i], columns[j])]
        scaled = [rows[i] * inverse[i] for i in range(8)]
        for u in below:
            for i in range(8):
                tiles[u] = tiles[u] - columns[i][u - t - 1] * scaled[i]
        done = rows[0] / jnp.sqrt(corner[0, 0])
        for i in range(1, 8):
            done = jnp.where(row == i, rows[i] / jnp.sqrt(corner[i, i]), done)
        tiles[t] = done
    return jnp.concatenate(tiles, axis=0)


def finish_kernel(sums_ref, parts_ref, modes_ref, proj_ref, corr_ref, held_ref, small_ref, sem):
    sums = sums_ref[...]
    inverse = inverse_factors(sums)
    own, following = inverse[:, M : 2 * M], inverse[:, 3 * M : 4 * M]
    group = iota((M, LANES), 1) // M
    wide = jnp.concatenate([own * math.sqrt(NX * NY)] * GROUPS, axis=1)
    wide = jnp.concatenate([jnp.where(group == g, wide, 0.0) for g in range(GROUPS)], axis=0)
    high, low = split(wide)
    stack = jnp.concatenate([high, high], axis=1)
    stack = jnp.concatenate([stack, jnp.concatenate([low, jnp.zeros_like(low)], axis=1)], axis=0)

    copies = []

    def send(source, target):
        copies.append(pltpu.make_async_copy(source, target, sem.at[len(copies)]))
        copies[-1].start()

    for half in range(2):
        rows = slice(8 * half, 8 * half + 8)
        for r in range(8 * half, 8 * half + 8):
            both = lax.dot_general(stack, parts_ref[r], (((1,), (1,)), ((), ())), preferred_element_type=F32)
            result = both[0:LANES] + both[LANES:]
            for g in range(GROUPS):
                held_ref[:, r, g * SPAN : (g + 1) * SPAN] = result[M * g : M * g + M]
        send(held_ref.at[:, rows], modes_ref.at[:, rows])

    exact = functools.partial(jnp.dot, precision=lax.Precision.HIGHEST, preferred_element_type=F32)
    image, across = sums[:, M : 2 * M], sums[:, 3 * M : 4 * M]
    small_ref[0] = exact(exact(own, image), own.T)
    has_next = lax.axis_index("slab") < lax.axis_size("slab") - 1
    small_ref[1] = jnp.where(has_next, exact(exact(own, across), following.T), 0.0)
    send(small_ref.at[0], proj_ref)
    send(small_ref.at[1], corr_ref)
    for copy in copies:
        copy.wait()


def add_over_strips(v):
    def others(x, *masks):
        return [lax.ppermute(x, "xs", [(i, i ^ mask) for i in range(64)]) for mask in masks]

    v = v + others(v, 1)[0]
    for unit in (2, 8):
        one, two, three = others(v, unit, 2 * unit, 3 * unit)
        v = (v + one) + (two + three)
    return v + others(v, 7 * 8)[0]


def local(perturbation, seeds):
    strips = NX // ROWS
    pert = perturbation[0]
    inner = lax.ppermute(pert, "xs", [(i, i ^ 1) for i in range(strips)])
    outer = lax.ppermute(pert, "xs", [(i, i - 1 if i % 2 == 0 else i + 1) for i in range(1, strips - 1)])
    vmem = pl.BlockSpec(memory_space=pltpu.VMEM)
    params = pltpu.CompilerParams(vmem_limit_bytes=28 * 2**20)
    strip = pl.pallas_call(
        assemble_kernel,
        name="assemble",
        out_shape=jax.ShapeDtypeStruct((32, NY), jnp.int32),
        in_specs=[vmem, vmem, vmem, vmem],
        out_specs=vmem,
        compiler_params=pltpu.CompilerParams(vmem_limit_bytes=4 * 2**20),
    )(inner, outer, pert, seeds[0].T)
    following = lax.ppermute(strip, "slab", [((i + 1) % 4, i) for i in range(4)])

    scratch = [
        pltpu.VMEM((EXT, STEPS, 8, LANES), F32),
        pltpu.VMEM((SPAN, LANES), F32),
        pltpu.VMEM((EXT, STEPS, 8, LANES), F32),
        pltpu.VMEM((EXT, STEPS, 8, LANES), F32),
    ]
    cost = pl.CostEstimate(flops=2**30, bytes_accessed=2**23, transcendentals=0)
    field, own = pl.pallas_call(
        own_kernel,
        name="own_trial",
        out_shape=(jax.ShapeDtypeStruct((ROWS * SPAN, LANES), F32), jax.ShapeDtypeStruct((M, 2 * M), F32)),
        in_specs=[vmem],
        out_specs=(vmem, vmem),
        scratch_shapes=scratch,
        compiler_params=params,
        cost_estimate=cost,
    )(strip)
    sums = pl.pallas_call(
        next_kernel,
        name="next_trial",
        out_shape=jax.ShapeDtypeStruct((M, 4 * M), F32),
        in_specs=[vmem, vmem, vmem],
        out_specs=vmem,
        scratch_shapes=scratch,
        compiler_params=params,
        cost_estimate=cost,
    )(following, field, own)
    parts = pl.pallas_call(
        parts_kernel,
        name="parts",
        out_shape=jax.ShapeDtypeStruct((ROWS, SPAN, 2 * LANES), BF16),
        in_specs=[vmem],
        out_specs=vmem,
        compiler_params=pltpu.CompilerParams(vmem_limit_bytes=12 * 2**20),
        cost_estimate=pl.CostEstimate(flops=2**20, bytes_accessed=2**22, transcendentals=0),
    )(field)
    sums = add_over_strips(sums)
    modes, projected, correlations = pl.pallas_call(
        finish_kernel,
        name="finish",
        out_shape=(
            jax.ShapeDtypeStruct((M, ROWS, NY), F32),
            jax.ShapeDtypeStruct((M, M), F32),
            jax.ShapeDtypeStruct((M, M), F32),
        ),
        in_specs=[vmem, vmem],
        out_specs=(pl.BlockSpec(memory_space=pl.ANY),) * 3,
        scratch_shapes=[
            pltpu.VMEM((M, ROWS, NY), F32),
            pltpu.VMEM((2, M, M), F32),
            pltpu.SemaphoreType.DMA((4,)),
        ],
        compiler_params=params,
        cost_estimate=pl.CostEstimate(flops=2**28, bytes_accessed=2**23, transcendentals=0),
    )(sums, parts)
    return modes[None], projected[None], correlations[None]


def solution(mesh):
    return jax.shard_map(
        local,
        mesh=mesh,
        in_specs=(P("slab", "xs", None), P("slab", None, None)),
        out_specs=(P("slab", None, "xs", None), P("slab", None, None), P("slab", None, None)),
        check_vma=False,
    )
```

```python
import functools
import math

import jax
import jax.numpy as jnp
from jax import lax
from jax.experimental import pallas as pl
from jax.experimental.pallas import tpu as pltpu
from jax.sharding import PartitionSpec as P

NX = 1024
NY = 1024
M = 32
ROWS = 16
HALO = 4
EXT = ROWS + 2 * HALO
LANES = 128
GROUPS = LANES // M
SPAN = NY // GROUPS
STEPS = SPAN // 8
F32 = jnp.float32
BF16 = jnp.bfloat16


def split(x):
    high = x.astype(BF16)
    return high, (x - high.astype(F32)).astype(BF16)


def iota(shape, axis):
    return lax.broadcasted_iota(jnp.int32, shape, axis)


def sine_tables(k, first, second):
    unit = math.pi / (NX + 1)
    base = column_base().astype(F32)
    scale = 2.0 / math.sqrt((NX + 1) * (NY + 1))
    angle = unit * second * (base + 1.0)
    sin_base, cos_base = scale * jnp.sin(angle), scale * jnp.cos(angle)
    step = unit * second * iota((STEPS, LANES), 0).astype(F32)
    sin_step, cos_step = jnp.sin(step), jnp.cos(step)
    sines = [sin_base * cos_step[q : q + 1] + cos_base * sin_step[q : q + 1] for q in range(STEPS)]
    row = iota((EXT, LANES), 0) + (k * ROWS - HALO)
    along_x = jnp.sin(unit * first * (row.astype(F32) + 1.0))
    along_x = jnp.where((row >= 0) & (row < NX), along_x, 0.0)
    return sines, along_x, 2.0 * jnp.cos(unit * first) + 2.0 * jnp.cos(unit * second)


def column_base():
    return iota((8, LANES), 1) // M * SPAN + iota((8, LANES), 0) * STEPS


def prepare_kernel(pert_ref, seeds_ref, strip_ref, sines_ref, along_ref, shift_ref):
    strip_ref[HALO : HALO + ROWS, :] = pert_ref[...]
    indices = jnp.concatenate([seeds_ref[...]] * GROUPS, axis=1)
    strip_ref[EXT : EXT + 2, 0:LANES] = indices
    first, second = indices[0:1].astype(F32), indices[1:2].astype(F32)
    sines, along_ref[...], shift = sine_tables(lax.axis_index("xs"), first, second)
    for q in range(STEPS):
        sines_ref[q] = sines[q]
    shift_ref[...] = jnp.broadcast_to(shift, (8, LANES))


def assemble_kernel(inner_ref, outer_ref, middle_ref, strip_ref):
    even = lax.axis_index("xs") % 2 == 0
    strip_ref[...] = middle_ref[...]
    strip_ref[0:HALO, :] = jnp.where(even, outer_ref[ROWS - HALO :, :], inner_ref[ROWS - HALO :, :])
    strip_ref[HALO + ROWS : EXT, :] = jnp.where(even, inner_ref[:HALO, :], outer_ref[:HALO, :])


def first_trial(k, strip_ref, sines, along_x, shift, w_ref, pert_ref, out_ref):
    xpos = ((iota((EXT, LANES), 0) + (k * ROWS - HALO)).astype(F32) + 0.5) / NX - 0.5
    x_part = 9.0 - 4.0 * (xpos * xpos + 0.5 * xpos)
    pert = strip_ref[0:EXT, :].astype(F32)
    stacked = [pert[:, g * SPAN : (g + 1) * SPAN] for g in range(GROUPS)]
    stacked = jnp.concatenate(stacked + [jnp.zeros((LANES - GROUPS * EXT, SPAN), F32)], axis=0)
    pert_ref[...] = jnp.transpose(stacked)
    spread = jnp.concatenate([pert_ref[pl.ds(q, 8, stride=STEPS), :] for q in range(STEPS)], axis=0).astype(BF16)
    source = iota((LANES, LANES), 0) - EXT * (iota((LANES, LANES), 1) // M)

    base = column_base().astype(F32)
    y_parts = []
    for q in range(STEPS):
        ypos = (base + (q + 0.5)) / NY - 0.5
        y_parts.append(2.4 * ypos * ypos)
    for r in range(EXT):
        here = jnp.dot(spread, (source == r).astype(BF16), preferred_element_type=F32)
        x_row = jnp.broadcast_to(x_part[r : r + 1], (8, LANES))
        sine_row = jnp.broadcast_to(along_x[r : r + 1], (8, LANES))
        for q in range(STEPS):
            w = (x_row - y_parts[q]) - 0.1 * here[8 * q : 8 * q + 8]
            w_ref[r, q] = w
            out_ref[r, q] = (w + shift) * (sine_row * sines[q])


def beyond(row_first, row_last):
    s, lane = iota((8, LANES), 0), iota((8, LANES), 1)
    down = pltpu.roll(row_last, 1, 0)
    left = jnp.where(s == 0, jnp.where(lane < M, 0.0, pltpu.roll(down, M, 1)), down)
    up = pltpu.roll(row_first, 7, 0)
    right = jnp.where(s == 7, jnp.where(lane >= LANES - M, 0.0, pltpu.roll(up, LANES - M, 1)), up)
    return left, right


def sweep(k, first_row, count, in_ref, w_ref, out_ref, shifted=0, hamiltonian=False):
    batch, chunk = count // 2, 4

    def rows(i, carry):
        r = first_row + i * batch
        ends = [beyond(in_ref[r + j, 0], in_ref[r + j, STEPS - 1]) for j in range(batch)]
        factor = {}
        top, bottom = HALO - 1 - first_row, EXT - HALO - first_row - batch
        if 0 <= top < batch:
            factor[top] = jnp.where((i == 0) & (k == 0), 0.0, 1.0)
        if 0 <= bottom < batch:
            factor[bottom] = jnp.where((i == 1) & (k == NX // ROWS - 1), 0.0, 1.0) * factor.get(bottom, 1.0)
        for q0 in range(0, STEPS, chunk):
            inside = range(q0, q0 + chunk)
            x = {(j, q): in_ref[r + j, q] for j in range(-1, batch + 1) for q in inside}
            for j in range(batch):
                x[j, q0 - 1] = in_ref[r + j, q0 - 1] if q0 > 0 else ends[j][0]
                x[j, q0 + chunk] = in_ref[r + j, q0 + chunk] if q0 + chunk < STEPS else ends[j][1]
            for j in range(batch):
                for q in inside:
                    near = (x[j, q - 1] + x[j, q + 1]) + (x[j - 1, q] + x[j + 1, q])
                    if hamiltonian:
                        value = (13.0 - w_ref[r + j, q]) * x[j, q] - near
                    else:
                        value = w_ref[r + j, q] * x[j, q] + near
                    if j in factor:
                        value = value * factor[j]
                    out_ref[r + j - shifted, q] = value
        return carry

    lax.fori_loop(0, 2, rows, 0)


def blocks(product):
    return sum(product[M * g : M * g + M, M * g : M * g + M] for g in range(GROUPS))


def dot_cells(a, b):
    return lax.dot_general(a, b, (((0,), (0,)), ((), ())), preferred_element_type=F32)


def own_kernel(
    strip_ref, sines_ref, along_ref, shift_ref, modes_ref, sums_ref, w_ref, pert_ref, one_ref, two_ref
):
    k = lax.axis_index("xs")
    sines = [sines_ref[q] for q in range(STEPS)]
    first_trial(k, strip_ref, sines, along_ref[...], shift_ref[...], w_ref, pert_ref, one_ref)
    sweep(k, 1, EXT - 2, one_ref, w_ref, two_ref)
    sweep(k, 2, EXT - 4, two_ref, w_ref, one_ref)
    sweep(k, 3, EXT - 6, one_ref, w_ref, two_ref)
    sweep(k, 4, ROWS, two_ref, w_ref, one_ref, hamiltonian=True)
    field = two_ref[HALO : HALO + ROWS].reshape(ROWS * SPAN, LANES)
    image = one_ref[HALO : HALO + ROWS].reshape(ROWS * SPAN, LANES)
    modes_ref[...] = field
    high, low = split(field)
    image_high, image_low = split(image)
    main = dot_cells(high, jnp.concatenate([high, low, image_high, image_low], axis=1))
    rest = blocks(dot_cells(low, image_high))
    cross = blocks(main[:, LANES : 2 * LANES])
    gram = blocks(main[:, 0:LANES]) + (cross + cross.T)
    ham = blocks(main[:, 2 * LANES : 3 * LANES]) + (blocks(main[:, 3 * LANES :]) + rest)
    sums_ref[...] = jnp.concatenate([gram, ham], axis=1)


def next_kernel(strip_ref, modes_ref, own_ref, sums_ref, w_ref, pert_ref, one_ref, two_ref):
    k = lax.axis_index("xs")
    first = strip_ref[EXT : EXT + 1, 0:LANES].astype(F32)
    second = strip_ref[EXT + 1 : EXT + 2, 0:LANES].astype(F32)
    first_trial(k, strip_ref, *sine_tables(k, first, second), w_ref, pert_ref, one_ref)
    sweep(k, 2, EXT - 4, one_ref, w_ref, two_ref)
    sweep(k, 3, EXT - 6, two_ref, w_ref, one_ref)
    sweep(k, 4, ROWS, one_ref, w_ref, two_ref)
    field = two_ref[HALO : HALO + ROWS].reshape(ROWS * SPAN, LANES)
    high, low = split(field)
    own_high, own_low = split(modes_ref[...])
    main = dot_cells(jnp.concatenate([high, own_high], axis=1), jnp.concatenate([high, low], axis=1))
    rest = blocks(dot_cells(own_low, high))
    cross = blocks(main[0:LANES, LANES:])
    gram = blocks(main[0:LANES, 0:LANES]) + (cross + cross.T)
    across = blocks(main[LANES:, 0:LANES]) + (blocks(main[LANES:, LANES:]) + rest)
    sums_ref[...] = jnp.concatenate([own_ref[...], gram, across], axis=1)


def parts_kernel(modes_ref, parts_ref):
    def rows(i, carry):
        for j in range(4):
            r = i * 4 + j
            pieces = [
                modes_ref[pl.ds(r * SPAN + q * 8 + s, 8, stride=8), :] for s in range(8) for q in range(0, STEPS, 8)
            ]
            parts_ref[r] = jnp.concatenate(split(jnp.concatenate(pieces, axis=0)), axis=1)
        return carry

    lax.fori_loop(0, ROWS // 4, rows, 0)


def inverse_factors(sums):
    row, lane = iota((8, LANES), 0), iota((8, LANES), 1)
    start = lane // (2 * M) * (2 * M)
    tiles = [
        jnp.where((lane // M) % 2 == 0, sums[8 * t : 8 * t + 8], (lane % M == row + 8 * t).astype(F32))
        for t in range(M // 8)
    ]
    for t in range(M // 8):
        lanes = [start + (8 * t + i) for i in range(8)]
        below = range(t + 1, M // 8)
        columns = [[jnp.take_along_axis(tiles[u], lanes[i], axis=1) for u in below] for i in range(8)]
        rows = [jnp.broadcast_to(tiles[t][i : i + 1], (8, LANES)) for i in range(8)]
        corner = {(i, j): jnp.take_along_axis(rows[i], lanes[j], axis=1) for i in range(8) for j in range(i, 8)}
        inverse, factor = [], {}
        for i in range(8):
            inverse.append(1.0 / corner[i, i])
            for j in range(i + 1, 8):
                factor[j, i] = corner[i, j] * inverse[i]
            for j in range(i + 1, 8):
                for m in range(j, 8):
                    corner[j, m] = corner[j, m] - factor[j, i] * corner[i, m]
        for i in range(8):
            for j in range(i):
                rows[i] = rows[i] - factor[i, j] * rows[j]
                columns[i] = [c - factor[i, j] * p for c, p in zip(columns[i], columns[j])]
        scaled = [rows[i] * inverse[i] for i in range(8)]
        for u in below:
            for i in range(8):
                tiles[u] = tiles[u] - columns[i][u - t - 1] * scaled[i]
        done = rows[0] / jnp.sqrt(corner[0, 0])
        for i in range(1, 8):
            done = jnp.where(row == i, rows[i] / jnp.sqrt(corner[i, i]), done)
        tiles[t] = done
    return jnp.concatenate(tiles, axis=0)


def finish_kernel(sums_ref, parts_ref, modes_ref, proj_ref, corr_ref, held_ref, small_ref, sem):
    sums = sums_ref[...]
    inverse = inverse_factors(sums)
    own, following = inverse[:, M : 2 * M], inverse[:, 3 * M : 4 * M]
    group = iota((M, LANES), 1) // M
    wide = jnp.concatenate([own * math.sqrt(NX * NY)] * GROUPS, axis=1)
    wide = jnp.concatenate([jnp.where(group == g, wide, 0.0) for g in range(GROUPS)], axis=0)
    high, low = split(wide)
    stack = jnp.concatenate([high, high], axis=1)
    stack = jnp.concatenate([stack, jnp.concatenate([low, jnp.zeros_like(low)], axis=1)], axis=0)

    copies = []

    def send(source, target):
        copies.append(pltpu.make_async_copy(source, target, sem.at[len(copies)]))
        copies[-1].start()

    for half in range(2):
        rows = slice(8 * half, 8 * half + 8)
        for r in range(8 * half, 8 * half + 8):
            both = lax.dot_general(stack, parts_ref[r], (((1,), (1,)), ((), ())), preferred_element_type=F32)
            result = both[0:LANES] + both[LANES:]
            for g in range(GROUPS):
                held_ref[:, r, g * SPAN : (g + 1) * SPAN] = result[M * g : M * g + M]
        send(held_ref.at[:, rows], modes_ref.at[:, rows])

    exact = functools.partial(jnp.dot, precision=lax.Precision.HIGHEST, preferred_element_type=F32)
    image, across = sums[:, M : 2 * M], sums[:, 3 * M : 4 * M]
    small_ref[0] = exact(exact(own, image), own.T)
    has_next = lax.axis_index("slab") < lax.axis_size("slab") - 1
    small_ref[1] = jnp.where(has_next, exact(exact(own, across), following.T), 0.0)
    send(small_ref.at[0], proj_ref)
    send(small_ref.at[1], corr_ref)
    for copy in copies:
        copy.wait()


def add_over_strips(v):
    def others(x, *masks):
        return [lax.ppermute(x, "xs", [(i, i ^ mask) for i in range(64)]) for mask in masks]

    v = v + others(v, 1)[0]
    for unit in (2, 8):
        one, two, three = others(v, unit, 2 * unit, 3 * unit)
        v = (v + one) + (two + three)
    return v + others(v, 7 * 8)[0]


def local(perturbation, seeds):
    strips = NX // ROWS
    pert = perturbation[0]
    inner = lax.ppermute(pert, "xs", [(i, i ^ 1) for i in range(strips)])
    outer = lax.ppermute(pert, "xs", [(i, i - 1 if i % 2 == 0 else i + 1) for i in range(1, strips - 1)])
    vmem = pl.BlockSpec(memory_space=pltpu.VMEM)
    params = pltpu.CompilerParams(vmem_limit_bytes=28 * 2**20)
    middle, *tables = pl.pallas_call(
        prepare_kernel,
        name="prepare",
        out_shape=(
            jax.ShapeDtypeStruct((32, NY), jnp.int32),
            jax.ShapeDtypeStruct((STEPS, 8, LANES), F32),
            jax.ShapeDtypeStruct((EXT, LANES), F32),
            jax.ShapeDtypeStruct((8, LANES), F32),
        ),
        in_specs=[vmem, vmem],
        out_specs=(vmem,) * 4,
        compiler_params=pltpu.CompilerParams(vmem_limit_bytes=4 * 2**20),
        cost_estimate=pl.CostEstimate(flops=2**20, bytes_accessed=2**20, transcendentals=2**14),
    )(pert, seeds[0].T)
    strip = pl.pallas_call(
        assemble_kernel,
        name="assemble",
        out_shape=jax.ShapeDtypeStruct((32, NY), jnp.int32),
        in_specs=[vmem, vmem, vmem],
        out_specs=vmem,
        compiler_params=pltpu.CompilerParams(vmem_limit_bytes=4 * 2**20),
    )(inner, outer, middle)
    following = lax.ppermute(strip, "slab", [((i + 1) % 4, i) for i in range(4)])

    scratch = [
        pltpu.VMEM((EXT, STEPS, 8, LANES), F32),
        pltpu.VMEM((SPAN, LANES), F32),
        pltpu.VMEM((EXT, STEPS, 8, LANES), F32),
        pltpu.VMEM((EXT, STEPS, 8, LANES), F32),
    ]
    cost = pl.CostEstimate(flops=2**30, bytes_accessed=2**23, transcendentals=0)
    field, own = pl.pallas_call(
        own_kernel,
        name="own_trial",
        out_shape=(jax.ShapeDtypeStruct((ROWS * SPAN, LANES), F32), jax.ShapeDtypeStruct((M, 2 * M), F32)),
        in_specs=[vmem, vmem, vmem, vmem],
        out_specs=(vmem, vmem),
        scratch_shapes=scratch,
        compiler_params=params,
        cost_estimate=cost,
    )(strip, *tables)
    sums = pl.pallas_call(
        next_kernel,
        name="next_trial",
        out_shape=jax.ShapeDtypeStruct((M, 4 * M), F32),
        in_specs=[vmem, vmem, vmem],
        out_specs=vmem,
        scratch_shapes=scratch,
        compiler_params=params,
        cost_estimate=cost,
    )(following, field, own)
    parts = pl.pallas_call(
        parts_kernel,
        name="parts",
        out_shape=jax.ShapeDtypeStruct((ROWS, SPAN, 2 * LANES), BF16),
        in_specs=[vmem],
        out_specs=vmem,
        compiler_params=pltpu.CompilerParams(vmem_limit_bytes=12 * 2**20),
        cost_estimate=pl.CostEstimate(flops=2**20, bytes_accessed=2**22, transcendentals=0),
    )(field)
    sums = add_over_strips(sums)
    modes, projected, correlations = pl.pallas_call(
        finish_kernel,
        name="finish",
        out_shape=(
            jax.ShapeDtypeStruct((M, ROWS, NY), F32),
            jax.ShapeDtypeStruct((M, M), F32),
            jax.ShapeDtypeStruct((M, M), F32),
        ),
        in_specs=[vmem, vmem],
        out_specs=(pl.BlockSpec(memory_space=pl.ANY),) * 3,
        scratch_shapes=[
            pltpu.VMEM((M, ROWS, NY), F32),
            pltpu.VMEM((2, M, M), F32),
            pltpu.SemaphoreType.DMA((4,)),
        ],
        compiler_params=params,
        cost_estimate=pl.CostEstimate(flops=2**28, bytes_accessed=2**23, transcendentals=0),
    )(sums, parts)
    return modes[None], projected[None], correlations[None]


def solution(mesh):
    return jax.shard_map(
        local,
        mesh=mesh,
        in_specs=(P("slab", "xs", None), P("slab", None, None)),
        out_specs=(P("slab", None, "xs", None), P("slab", None, None), P("slab", None, None)),
        check_vma=False,
    )
```

```python
import functools
import math

import jax
import jax.numpy as jnp
from jax import lax
from jax.experimental import pallas as pl
from jax.experimental.pallas import tpu as pltpu
from jax.sharding import PartitionSpec as P

NX = 1024
NY = 1024
M = 32
ROWS = 16
HALO = 4
EXT = ROWS + 2 * HALO
LANES = 128
GROUPS = LANES // M
SPAN = NY // GROUPS
STEPS = SPAN // 8
SENT = EXT
F32 = jnp.float32
BF16 = jnp.bfloat16


def split(x):
    high = x.astype(BF16)
    return high, (x - high.astype(F32)).astype(BF16)


def iota(shape, axis):
    return lax.broadcasted_iota(jnp.int32, shape, axis)


def sine_tables(k, first, second):
    unit = math.pi / (NX + 1)
    base = column_base().astype(F32)
    scale = 2.0 / math.sqrt((NX + 1) * (NY + 1))
    angle = unit * second * (base + 1.0)
    sin_base, cos_base = scale * jnp.sin(angle), scale * jnp.cos(angle)
    step = unit * second * iota((STEPS, LANES), 0).astype(F32)
    sin_step, cos_step = jnp.sin(step), jnp.cos(step)
    sines = [sin_base * cos_step[q : q + 1] + cos_base * sin_step[q : q + 1] for q in range(STEPS)]
    row = iota((EXT, LANES), 0) + (k * ROWS - HALO)
    along_x = jnp.sin(unit * first * (row.astype(F32) + 1.0))
    along_x = jnp.where((row >= 0) & (row < NX), along_x, 0.0)
    return sines, along_x, 2.0 * jnp.cos(unit * first) + 2.0 * jnp.cos(unit * second)


def column_base():
    return iota((8, LANES), 1) // M * SPAN + iota((8, LANES), 0) * STEPS


def first_rows(k, pert, rows, sines, along_x, shift, turned_ref, write):
    count = pert.shape[0]
    xpos = ((iota((EXT, LANES), 0) + (k * ROWS - HALO)).astype(F32) + 0.5) / NX - 0.5
    x_part = 9.0 - 4.0 * (xpos * xpos + 0.5 * xpos)
    stacked = [pert[:, g * SPAN : (g + 1) * SPAN] for g in range(GROUPS)]
    stacked = jnp.concatenate(stacked + [jnp.zeros((LANES - GROUPS * count, SPAN), F32)], axis=0)
    turned_ref[...] = jnp.transpose(stacked)
    spread = jnp.concatenate([turned_ref[pl.ds(q, 8, stride=STEPS), :] for q in range(STEPS)], axis=0).astype(BF16)
    source = iota((LANES, LANES), 0) - count * (iota((LANES, LANES), 1) // M)

    base = column_base().astype(F32)
    y_parts = []
    for q in range(STEPS):
        ypos = (base + (q + 0.5)) / NY - 0.5
        y_parts.append(2.4 * ypos * ypos)
    for i, e in rows:
        here = jnp.dot(spread, (source == i).astype(BF16), preferred_element_type=F32)
        x_row = jnp.broadcast_to(x_part[e : e + 1], (8, LANES))
        sine_row = jnp.broadcast_to(along_x[e : e + 1], (8, LANES))
        for q in range(STEPS):
            w = (x_row - y_parts[q]) - 0.1 * here[8 * q : 8 * q + 8]
            write(i, e, q, w, (w + shift) * (sine_row * sines[q]))


def prepare_kernel(
    pert_hbm, seeds_hbm, strip_ref, sines_ref, along_ref, shift_ref, w_ref, out_ref, pert_ref, seeds_ref, turned_ref, sem
):
    k = lax.axis_index("xs")
    pert_copy = pltpu.make_async_copy(pert_hbm, pert_ref, sem.at[0])
    seeds_copy = pltpu.make_async_copy(seeds_hbm, seeds_ref, sem.at[1])
    pert_copy.start()
    seeds_copy.start()
    seeds_copy.wait()
    indices = jnp.concatenate([seeds_ref[...]] * GROUPS, axis=1)
    first, second = indices[0:1].astype(F32), indices[1:2].astype(F32)
    sines, along_x, shift = sine_tables(k, first, second)
    for q in range(STEPS):
        sines_ref[q] = sines[q]
    along_ref[...] = along_x
    shift_ref[...] = jnp.broadcast_to(shift, (8, LANES))
    strip_ref[SENT - 2 : SENT - 1, 0:LANES] = indices[0:1]
    strip_ref[SENT - 2 : SENT - 1, LANES : 2 * LANES] = indices[1:2]
    pert_copy.wait()
    strip_ref[HALO - 1 : HALO - 1 + ROWS, :] = pert_ref[...]

    def write(i, e, q, w, value):
        w_ref[i, q] = w
        out_ref[i, q] = value

    rows = [(i, i + HALO) for i in range(ROWS)]
    first_rows(k, pert_ref[...].astype(F32), rows, sines, along_x, shift, turned_ref, write)


def halo(inner_ref, outer_ref):
    even = lax.axis_index("xs") % 2 == 0
    before = jnp.where(even, outer_ref[ROWS - HALO :, :], inner_ref[ROWS - HALO :, :])
    after = jnp.where(even, inner_ref[:HALO, :], outer_ref[:HALO, :])
    return before, after


def assemble_kernel(inner_ref, outer_ref, middle_ref, strip_ref):
    before, after = halo(inner_ref, outer_ref)
    strip_ref[...] = middle_ref[...]
    strip_ref[0 : HALO - 1, :] = before[1:]
    strip_ref[HALO - 1 + ROWS : SENT - 2, :] = after[: HALO - 1]


def beyond(row_first, row_last):
    s, lane = iota((8, LANES), 0), iota((8, LANES), 1)
    down = pltpu.roll(row_last, 1, 0)
    left = jnp.where(s == 0, jnp.where(lane < M, 0.0, pltpu.roll(down, M, 1)), down)
    up = pltpu.roll(row_first, 7, 0)
    right = jnp.where(s == 7, jnp.where(lane >= LANES - M, 0.0, pltpu.roll(up, LANES - M, 1)), up)
    return left, right


def strip_row(i, j):
    return j + i * (EXT - 1 - 2 * j)


def whole(ref):
    return lambda i, j, q: ref[strip_row(i, j), q]


def parted(halo_ref, own_ref):
    def get(i, j, q):
        if j < HALO:
            return halo_ref[j + i * (2 * HALO - 1 - 2 * j), q]
        return own_ref[strip_row(i, j) - HALO, q]

    return get


def sweep(k, margin, source, weight, out_ref, hamiltonian=False):
    first, stop, chunk = HALO - margin, EXT // 2, 4

    def half(i, carry):
        ends = {j: beyond(source(i, j, 0), source(i, j, STEPS - 1)) for j in range(first, stop)}
        inside_grid = jnp.where(k == i * (NX // ROWS - 1), 0.0, 1.0)
        for q0 in range(0, STEPS, chunk):
            inside = range(q0, q0 + chunk)
            x = {(j, q): source(i, j, q) for j in range(first - 1, stop + 1) for q in inside}
            for j in range(first, stop):
                x[j, q0 - 1] = source(i, j, q0 - 1) if q0 > 0 else ends[j][0]
                x[j, q0 + chunk] = source(i, j, q0 + chunk) if q0 + chunk < STEPS else ends[j][1]
            for j in range(first, stop):
                for q in inside:
                    near = (x[j, q - 1] + x[j, q + 1]) + (x[j - 1, q] + x[j + 1, q])
                    if hamiltonian:
                        value = (13.0 - weight(i, j, q)) * x[j, q] - near
                    else:
                        value = weight(i, j, q) * x[j, q] + near
                    if j == HALO - 1:
                        value = value * inside_grid
                    out_ref[strip_row(i, j), q] = value
        return carry

    lax.fori_loop(0, 2, half, 0)


def blocks(product):
    return sum(product[M * g : M * g + M, M * g : M * g + M] for g in range(GROUPS))


def dot_cells(a, b):
    return lax.dot_general(a, b, (((0,), (0,)), ((), ())), preferred_element_type=F32)


def own_kernel(
    inner_ref, outer_ref, sines_ref, along_ref, shift_ref, w_ref, first_ref,
    modes_ref, sums_ref, halo_w_ref, halo_ref, turned_ref, one_ref, two_ref,
):
    k = lax.axis_index("xs")

    def write(i, e, q, w, value):
        halo_w_ref[i, q] = w
        halo_ref[i, q] = value

    pert = jnp.concatenate(halo(inner_ref, outer_ref), axis=0).astype(F32)
    rows = [(i, i if i < HALO else i + ROWS) for i in range(2 * HALO)]
    sines = [sines_ref[q] for q in range(STEPS)]
    first_rows(k, pert, rows, sines, along_ref[...], shift_ref[...], turned_ref, write)
    weight = parted(halo_w_ref, w_ref)
    sweep(k, 3, parted(halo_ref, first_ref), weight, two_ref)
    sweep(k, 2, whole(two_ref), weight, one_ref)
    sweep(k, 1, whole(one_ref), weight, two_ref)
    sweep(k, 0, whole(two_ref), weight, one_ref, hamiltonian=True)
    field = two_ref[HALO : HALO + ROWS].reshape(ROWS * SPAN, LANES)
    image = one_ref[HALO : HALO + ROWS].reshape(ROWS * SPAN, LANES)
    modes_ref[...] = field
    high, low = split(field)
    image_high, image_low = split(image)
    main = dot_cells(high, jnp.concatenate([high, low, image_high, image_low], axis=1))
    rest = blocks(dot_cells(low, image_high))
    cross = blocks(main[:, LANES : 2 * LANES])
    gram = blocks(main[:, 0:LANES]) + (cross + cross.T)
    ham = blocks(main[:, 2 * LANES : 3 * LANES]) + (blocks(main[:, 3 * LANES :]) + rest)
    sums_ref[...] = jnp.concatenate([gram, ham], axis=1)


def next_kernel(strip_ref, modes_ref, own_ref, sums_ref, w_ref, turned_ref, one_ref, two_ref):
    k = lax.axis_index("xs")
    first = strip_ref[SENT - 2 : SENT - 1, 0:LANES].astype(F32)
    second = strip_ref[SENT - 2 : SENT - 1, LANES : 2 * LANES].astype(F32)

    def write(i, e, q, w, value):
        w_ref[e, q] = w
        one_ref[e, q] = value

    rows = [(i, i + 1) for i in range(EXT - 2)]
    first_rows(k, strip_ref[...].astype(F32), rows, *sine_tables(k, first, second), turned_ref, write)
    weight = whole(w_ref)
    sweep(k, 2, whole(one_ref), weight, two_ref)
    sweep(k, 1, whole(two_ref), weight, one_ref)
    sweep(k, 0, whole(one_ref), weight, two_ref)
    field = two_ref[HALO : HALO + ROWS].reshape(ROWS * SPAN, LANES)
    high, low = split(field)
    own_high, own_low = split(modes_ref[...])
    main = dot_cells(jnp.concatenate([high, own_high], axis=1), jnp.concatenate([high, low], axis=1))
    rest = blocks(dot_cells(own_low, high))
    cross = blocks(main[0:LANES, LANES:])
    gram = blocks(main[0:LANES, 0:LANES]) + (cross + cross.T)
    across = blocks(main[LANES:, 0:LANES]) + (blocks(main[LANES:, LANES:]) + rest)
    sums_ref[...] = jnp.concatenate([own_ref[...], gram, across], axis=1)


def parts_kernel(modes_ref, parts_ref):
    def rows(i, carry):
        for j in range(4):
            r = i * 4 + j
            pieces = [
                modes_ref[pl.ds(r * SPAN + q * 8 + s, 8, stride=8), :] for s in range(8) for q in range(0, STEPS, 8)
            ]
            parts_ref[r] = jnp.concatenate(split(jnp.concatenate(pieces, axis=0)), axis=1)
        return carry

    lax.fori_loop(0, ROWS // 4, rows, 0)


def inverse_factors(sums):
    row, lane = iota((8, LANES), 0), iota((8, LANES), 1)
    start = lane // (2 * M) * (2 * M)
    tiles = [
        jnp.where((lane // M) % 2 == 0, sums[8 * t : 8 * t + 8], (lane % M == row + 8 * t).astype(F32))
        for t in range(M // 8)
    ]
    for t in range(M // 8):
        lanes = [start + (8 * t + i) for i in range(8)]
        below = range(t + 1, M // 8)
        columns = [[jnp.take_along_axis(tiles[u], lanes[i], axis=1) for u in below] for i in range(8)]
        rows = [jnp.broadcast_to(tiles[t][i : i + 1], (8, LANES)) for i in range(8)]
        corner = {(i, j): jnp.take_along_axis(rows[i], lanes[j], axis=1) for i in range(8) for j in range(i, 8)}
        inverse, factor = [], {}
        for i in range(8):
            inverse.append(1.0 / corner[i, i])
            for j in range(i + 1, 8):
                factor[j, i] = corner[i, j] * inverse[i]
            for j in range(i + 1, 8):
                for m in range(j, 8):
                    corner[j, m] = corner[j, m] - factor[j, i] * corner[i, m]
        for i in range(8):
            for j in range(i):
                rows[i] = rows[i] - factor[i, j] * rows[j]
                columns[i] = [c - factor[i, j] * p for c, p in zip(columns[i], columns[j])]
        scaled = [rows[i] * inverse[i] for i in range(8)]
        for u in below:
            for i in range(8):
                tiles[u] = tiles[u] - columns[i][u - t - 1] * scaled[i]
        done = rows[0] / jnp.sqrt(corner[0, 0])
        for i in range(1, 8):
            done = jnp.where(row == i, rows[i] / jnp.sqrt(corner[i, i]), done)
        tiles[t] = done
    return jnp.concatenate(tiles, axis=0)


def finish_kernel(sums_ref, parts_ref, modes_ref, proj_ref, corr_ref, held_ref, small_ref, sem):
    sums = sums_ref[...]
    inverse = inverse_factors(sums)
    own, following = inverse[:, M : 2 * M], inverse[:, 3 * M : 4 * M]
    group = iota((M, LANES), 1) // M
    wide = jnp.concatenate([own * math.sqrt(NX * NY)] * GROUPS, axis=1)
    wide = jnp.concatenate([jnp.where(group == g, wide, 0.0) for g in range(GROUPS)], axis=0)
    high, low = split(wide)
    stack = jnp.concatenate([high, high], axis=1)
    stack = jnp.concatenate([stack, jnp.concatenate([low, jnp.zeros_like(low)], axis=1)], axis=0)

    copies = []

    def send(source, target):
        copies.append(pltpu.make_async_copy(source, target, sem.at[len(copies)]))
        copies[-1].start()

    for half in range(2):
        rows = slice(8 * half, 8 * half + 8)
        for r in range(8 * half, 8 * half + 8):
            both = lax.dot_general(stack, parts_ref[r], (((1,), (1,)), ((), ())), preferred_element_type=F32)
            result = both[0:LANES] + both[LANES:]
            for g in range(GROUPS):
                held_ref[:, r, g * SPAN : (g + 1) * SPAN] = result[M * g : M * g + M]
        send(held_ref.at[:, rows], modes_ref.at[:, rows])

    exact = functools.partial(jnp.dot, precision=lax.Precision.HIGHEST, preferred_element_type=F32)
    image, across = sums[:, M : 2 * M], sums[:, 3 * M : 4 * M]
    small_ref[0] = exact(exact(own, image), own.T)
    has_next = lax.axis_index("slab") < lax.axis_size("slab") - 1
    small_ref[1] = jnp.where(has_next, exact(exact(own, across), following.T), 0.0)
    send(small_ref.at[0], proj_ref)
    send(small_ref.at[1], corr_ref)
    for copy in copies:
        copy.wait()


def add_over_strips(v):
    def others(x, *masks):
        return [lax.ppermute(x, "xs", [(i, i ^ mask) for i in range(64)]) for mask in masks]

    v = v + others(v, 1)[0]
    for unit in (2, 8):
        one, two, three = others(v, unit, 2 * unit, 3 * unit)
        v = (v + one) + (two + three)
    return v + others(v, 7 * 8)[0]


def local(perturbation, seeds):
    strips = NX // ROWS
    pert = perturbation[0]
    inner = lax.ppermute(pert, "xs", [(i, i ^ 1) for i in range(strips)])
    outer = lax.ppermute(pert, "xs", [(i, i - 1 if i % 2 == 0 else i + 1) for i in range(1, strips - 1)])
    vmem = pl.BlockSpec(memory_space=pltpu.VMEM)
    params = pltpu.CompilerParams(vmem_limit_bytes=28 * 2**20)
    field_shape = (STEPS, 8, LANES)
    middle, *tables = pl.pallas_call(
        prepare_kernel,
        name="prepare",
        out_shape=(
            jax.ShapeDtypeStruct((SENT, NY), jnp.int32),
            jax.ShapeDtypeStruct(field_shape, F32),
            jax.ShapeDtypeStruct((EXT, LANES), F32),
            jax.ShapeDtypeStruct((8, LANES), F32),
            jax.ShapeDtypeStruct((ROWS, *field_shape), F32),
            jax.ShapeDtypeStruct((ROWS, *field_shape), F32),
        ),
        in_specs=[pl.BlockSpec(memory_space=pltpu.HBM)] * 2,
        out_specs=(vmem,) * 6,
        scratch_shapes=[
            pltpu.VMEM((ROWS, NY), jnp.int32),
            pltpu.VMEM((2, M), jnp.int32),
            pltpu.VMEM((SPAN, LANES), F32),
            pltpu.SemaphoreType.DMA((2,)),
        ],
        compiler_params=pltpu.CompilerParams(vmem_limit_bytes=12 * 2**20),
        cost_estimate=pl.CostEstimate(flops=2**26, bytes_accessed=2**22, transcendentals=2**14),
    )(pert, seeds[0].T)
    strip = pl.pallas_call(
        assemble_kernel,
        name="assemble",
        out_shape=jax.ShapeDtypeStruct((SENT, NY), jnp.int32),
        in_specs=[vmem, vmem, vmem],
        out_specs=vmem,
        compiler_params=pltpu.CompilerParams(vmem_limit_bytes=4 * 2**20),
    )(inner, outer, middle)
    following = lax.ppermute(strip, "slab", [((i + 1) % 4, i) for i in range(4)])

    trial = pltpu.VMEM((EXT, *field_shape), F32)
    edges = pltpu.VMEM((2 * HALO, *field_shape), F32)
    turned = pltpu.VMEM((SPAN, LANES), F32)
    cost = pl.CostEstimate(flops=2**30, bytes_accessed=2**23, transcendentals=0)
    field, own = pl.pallas_call(
        own_kernel,
        name="own_trial",
        out_shape=(jax.ShapeDtypeStruct((ROWS * SPAN, LANES), F32), jax.ShapeDtypeStruct((M, 2 * M), F32)),
        in_specs=[vmem] * 7,
        out_specs=(vmem, vmem),
        scratch_shapes=[edges, edges, turned, trial, trial],
        compiler_params=params,
        cost_estimate=cost,
    )(inner, outer, *tables)
    sums = pl.pallas_call(
        next_kernel,
        name="next_trial",
        out_shape=jax.ShapeDtypeStruct((M, 4 * M), F32),
        in_specs=[vmem, vmem, vmem],
        out_specs=vmem,
        scratch_shapes=[trial, turned, trial, trial],
        compiler_params=params,
        cost_estimate=cost,
    )(following, field, own)
    parts = pl.pallas_call(
        parts_kernel,
        name="parts",
        out_shape=jax.ShapeDtypeStruct((ROWS, SPAN, 2 * LANES), BF16),
        in_specs=[vmem],
        out_specs=vmem,
        compiler_params=pltpu.CompilerParams(vmem_limit_bytes=12 * 2**20),
        cost_estimate=pl.CostEstimate(flops=2**20, bytes_accessed=2**22, transcendentals=0),
    )(field)
    sums = add_over_strips(sums)
    modes, projected, correlations = pl.pallas_call(
        finish_kernel,
        name="finish",
        out_shape=(
            jax.ShapeDtypeStruct((M, ROWS, NY), F32),
            jax.ShapeDtypeStruct((M, M), F32),
            jax.ShapeDtypeStruct((M, M), F32),
        ),
        in_specs=[vmem, vmem],
        out_specs=(pl.BlockSpec(memory_space=pl.ANY),) * 3,
        scratch_shapes=[
            pltpu.VMEM((M, ROWS, NY), F32),
            pltpu.VMEM((2, M, M), F32),
            pltpu.SemaphoreType.DMA((4,)),
        ],
        compiler_params=params,
        cost_estimate=pl.CostEstimate(flops=2**28, bytes_accessed=2**23, transcendentals=0),
    )(sums, parts)
    return modes[None], projected[None], correlations[None]


def solution(mesh):
    return jax.shard_map(
        local,
        mesh=mesh,
        in_specs=(P("slab", "xs", None), P("slab", None, None)),
        out_specs=(P("slab", None, "xs", None), P("slab", None, None), P("slab", None, None)),
        check_vma=False,
    )
```

```python
import functools
import math

import jax
import jax.numpy as jnp
from jax import lax
from jax.experimental import pallas as pl
from jax.experimental.pallas import tpu as pltpu
from jax.sharding import PartitionSpec as P

NX = 1024
NY = 1024
M = 32
ROWS = 16
HALO = 4
EXT = ROWS + 2 * HALO
LANES = 128
GROUPS = LANES // M
SPAN = NY // GROUPS
STEPS = SPAN // 8
SENT = EXT
F32 = jnp.float32
BF16 = jnp.bfloat16


def split(x):
    high = x.astype(BF16)
    return high, (x - high.astype(F32)).astype(BF16)


def iota(shape, axis):
    return lax.broadcasted_iota(jnp.int32, shape, axis)


def sine_tables(k, first, second):
    unit = math.pi / (NX + 1)
    base = column_base().astype(F32)
    scale = 2.0 / math.sqrt((NX + 1) * (NY + 1))
    angle = unit * second * (base + 1.0)
    sin_base, cos_base = scale * jnp.sin(angle), scale * jnp.cos(angle)
    step = unit * second * iota((STEPS, LANES), 0).astype(F32)
    sin_step, cos_step = jnp.sin(step), jnp.cos(step)
    sines = [sin_base * cos_step[q : q + 1] + cos_base * sin_step[q : q + 1] for q in range(STEPS)]
    row = iota((EXT, LANES), 0) + (k * ROWS - HALO)
    along_x = jnp.sin(unit * first * (row.astype(F32) + 1.0))
    along_x = jnp.where((row >= 0) & (row < NX), along_x, 0.0)
    return sines, along_x, 2.0 * jnp.cos(unit * first) + 2.0 * jnp.cos(unit * second)


def column_base():
    return iota((8, LANES), 1) // M * SPAN + iota((8, LANES), 0) * STEPS


def first_rows(k, pert, rows, sines, along_x, shift, turned_ref, write):
    count = pert.shape[0]
    xpos = ((iota((EXT, LANES), 0) + (k * ROWS - HALO)).astype(F32) + 0.5) / NX - 0.5
    x_terms = thirds(10.0 * (9.0 - 4.0 * (xpos * xpos + 0.5 * xpos)))
    stacked = [pert[:, g * SPAN : (g + 1) * SPAN] for g in range(GROUPS)]
    stacked = jnp.concatenate(stacked + [jnp.zeros((LANES - GROUPS * count, SPAN), F32)], axis=0)
    turned_ref[...] = jnp.transpose(stacked)

    lane, s = iota((8, LANES), 1), iota((8, LANES), 0)
    term = lane % 4
    base = ((lane - 96) // 4 * SPAN + s * STEPS).astype(F32)
    spread = []
    for q in range(STEPS):
        ypos = (base + (q + 0.5)) / NY - 0.5
        one, two, three = thirds(24.0 * ypos * ypos)
        y_terms = jnp.where(term == 0, one, jnp.where(term == 1, two, jnp.where(term == 2, three, 0.0)))
        extra = jnp.where(lane < 96, 0.0, jnp.where(lane < 112, y_terms, jnp.where(lane < 115, 1.0, 0.0)))
        spread.append(turned_ref[pl.ds(q, 8, stride=STEPS), :] + extra)
    spread = jnp.concatenate(spread, axis=0).astype(BF16)

    line, group = iota((112, LANES), 0), iota((112, LANES), 1) // M
    source = line - count * group
    y_pick = jnp.where((line >= 96) & ((line - 96) // 4 == group), -1.0, 0.0)
    for i, e in rows:
        pick = jnp.where(source == i, -1.0, y_pick)
        parts = [jnp.broadcast_to(part[e : e + 1], (8, LANES)) for part in x_terms]
        x_pick = jnp.where(s == 0, parts[0], jnp.where(s == 1, parts[1], jnp.where(s == 2, parts[2], 0.0)))
        pick = jnp.concatenate([pick, x_pick, jnp.zeros((8, LANES), F32)], axis=0).astype(BF16)
        here = jnp.dot(spread, pick, preferred_element_type=F32)
        sine_row = jnp.broadcast_to(along_x[e : e + 1], (8, LANES))
        for q in range(STEPS):
            w = 0.1 * here[8 * q : 8 * q + 8]
            write(i, e, q, w, (w + shift) * (sine_row * sines[q]))


def thirds(x):
    one = x.astype(BF16).astype(F32)
    two = (x - one).astype(BF16).astype(F32)
    return one, two, (x - one) - two


def prepare_kernel(
    pert_hbm, seeds_hbm, strip_ref, sines_ref, along_ref, shift_ref, w_ref, out_ref, pert_ref, seeds_ref, turned_ref, sem
):
    k = lax.axis_index("xs")
    pert_copy = pltpu.make_async_copy(pert_hbm, pert_ref, sem.at[0])
    seeds_copy = pltpu.make_async_copy(seeds_hbm, seeds_ref, sem.at[1])
    pert_copy.start()
    seeds_copy.start()
    seeds_copy.wait()
    indices = jnp.concatenate([seeds_ref[...]] * GROUPS, axis=1)
    first, second = indices[0:1].astype(F32), indices[1:2].astype(F32)
    sines, along_x, shift = sine_tables(k, first, second)
    for q in range(STEPS):
        sines_ref[q] = sines[q]
    along_ref[...] = along_x
    shift_ref[...] = jnp.broadcast_to(shift, (8, LANES))
    strip_ref[SENT - 2 : SENT - 1, 0:LANES] = indices[0:1]
    strip_ref[SENT - 2 : SENT - 1, LANES : 2 * LANES] = indices[1:2]
    pert_copy.wait()
    strip_ref[HALO - 1 : HALO - 1 + ROWS, :] = pert_ref[...]

    def write(i, e, q, w, value):
        w_ref[i, q] = w
        out_ref[i, q] = value

    rows = [(i, i + HALO) for i in range(ROWS)]
    first_rows(k, pert_ref[...].astype(F32), rows, sines, along_x, shift, turned_ref, write)


def halo(inner_ref, outer_ref):
    even = lax.axis_index("xs") % 2 == 0
    before = jnp.where(even, outer_ref[ROWS - HALO :, :], inner_ref[ROWS - HALO :, :])
    after = jnp.where(even, inner_ref[:HALO, :], outer_ref[:HALO, :])
    return before, after


def assemble_kernel(inner_ref, outer_ref, middle_ref, strip_ref):
    before, after = halo(inner_ref, outer_ref)
    strip_ref[...] = middle_ref[...]
    strip_ref[0 : HALO - 1, :] = before[1:]
    strip_ref[HALO - 1 + ROWS : SENT - 2, :] = after[: HALO - 1]


def beyond(row_first, row_last):
    s, lane = iota((8, LANES), 0), iota((8, LANES), 1)
    down = pltpu.roll(row_last, 1, 0)
    left = jnp.where(s == 0, jnp.where(lane < M, 0.0, pltpu.roll(down, M, 1)), down)
    up = pltpu.roll(row_first, 7, 0)
    right = jnp.where(s == 7, jnp.where(lane >= LANES - M, 0.0, pltpu.roll(up, LANES - M, 1)), up)
    return left, right


def strip_row(i, j):
    return j + i * (EXT - 1 - 2 * j)


def whole(ref):
    return lambda i, j, q: ref[strip_row(i, j), q]


def parted(halo_ref, own_ref):
    def get(i, j, q):
        if j < HALO:
            return halo_ref[j + i * (2 * HALO - 1 - 2 * j), q]
        return own_ref[strip_row(i, j) - HALO, q]

    return get


def sweep(k, margin, source, weight, out_ref, hamiltonian=False):
    first, stop, chunk = HALO - margin, EXT // 2, 4

    def half(i, carry):
        ends = {j: beyond(source(i, j, 0), source(i, j, STEPS - 1)) for j in range(first, stop)}
        inside_grid = jnp.where(k == i * (NX // ROWS - 1), 0.0, 1.0)
        for q0 in range(0, STEPS, chunk):
            inside = range(q0, q0 + chunk)
            x = {(j, q): source(i, j, q) for j in range(first - 1, stop + 1) for q in inside}
            for j in range(first, stop):
                x[j, q0 - 1] = source(i, j, q0 - 1) if q0 > 0 else ends[j][0]
                x[j, q0 + chunk] = source(i, j, q0 + chunk) if q0 + chunk < STEPS else ends[j][1]
            for j in range(first, stop):
                for q in inside:
                    near = (x[j, q - 1] + x[j, q + 1]) + (x[j - 1, q] + x[j + 1, q])
                    if hamiltonian:
                        value = (13.0 - weight(i, j, q)) * x[j, q] - near
                    else:
                        value = weight(i, j, q) * x[j, q] + near
                    if j == HALO - 1:
                        value = value * inside_grid
                    out_ref[strip_row(i, j), q] = value
        return carry

    lax.fori_loop(0, 2, half, 0)


def blocks(product):
    return sum(product[M * g : M * g + M, M * g : M * g + M] for g in range(GROUPS))


def dot_cells(a, b):
    return lax.dot_general(a, b, (((0,), (0,)), ((), ())), preferred_element_type=F32)


def own_kernel(
    inner_ref, outer_ref, sines_ref, along_ref, shift_ref, w_ref, first_ref,
    modes_ref, sums_ref, halo_w_ref, halo_ref, turned_ref, one_ref, two_ref,
):
    k = lax.axis_index("xs")

    def write(i, e, q, w, value):
        halo_w_ref[i, q] = w
        halo_ref[i, q] = value

    pert = jnp.concatenate(halo(inner_ref, outer_ref), axis=0).astype(F32)
    rows = [(i, i if i < HALO else i + ROWS) for i in range(2 * HALO)]
    sines = [sines_ref[q] for q in range(STEPS)]
    first_rows(k, pert, rows, sines, along_ref[...], shift_ref[...], turned_ref, write)
    weight = parted(halo_w_ref, w_ref)
    sweep(k, 3, parted(halo_ref, first_ref), weight, two_ref)
    sweep(k, 2, whole(two_ref), weight, one_ref)
    sweep(k, 1, whole(one_ref), weight, two_ref)
    sweep(k, 0, whole(two_ref), weight, one_ref, hamiltonian=True)
    field = two_ref[HALO : HALO + ROWS].reshape(ROWS * SPAN, LANES)
    image = one_ref[HALO : HALO + ROWS].reshape(ROWS * SPAN, LANES)
    modes_ref[...] = field
    high, low = split(field)
    image_high, image_low = split(image)
    main = dot_cells(high, jnp.concatenate([high, low, image_high, image_low], axis=1))
    rest = blocks(dot_cells(low, image_high))
    cross = blocks(main[:, LANES : 2 * LANES])
    gram = blocks(main[:, 0:LANES]) + (cross + cross.T)
    ham = blocks(main[:, 2 * LANES : 3 * LANES]) + (blocks(main[:, 3 * LANES :]) + rest)
    sums_ref[...] = jnp.concatenate([gram, ham], axis=1)


def next_kernel(strip_ref, modes_ref, own_ref, sums_ref, w_ref, turned_ref, one_ref, two_ref):
    k = lax.axis_index("xs")
    first = strip_ref[SENT - 2 : SENT - 1, 0:LANES].astype(F32)
    second = strip_ref[SENT - 2 : SENT - 1, LANES : 2 * LANES].astype(F32)

    def write(i, e, q, w, value):
        w_ref[e, q] = w
        one_ref[e, q] = value

    rows = [(i, i + 1) for i in range(EXT - 2)]
    first_rows(k, strip_ref[...].astype(F32), rows, *sine_tables(k, first, second), turned_ref, write)
    weight = whole(w_ref)
    sweep(k, 2, whole(one_ref), weight, two_ref)
    sweep(k, 1, whole(two_ref), weight, one_ref)
    sweep(k, 0, whole(one_ref), weight, two_ref)
    field = two_ref[HALO : HALO + ROWS].reshape(ROWS * SPAN, LANES)
    high, low = split(field)
    own_high, own_low = split(modes_ref[...])
    main = dot_cells(high, jnp.concatenate([high, low, own_high, own_low], axis=1))
    rest = blocks(dot_cells(low, own_high))
    cross = blocks(main[:, LANES : 2 * LANES])
    gram = blocks(main[:, 0:LANES]) + (cross + cross.T)
    across = blocks(main[:, 2 * LANES : 3 * LANES]) + (blocks(main[:, 3 * LANES :]) + rest)
    sums_ref[...] = jnp.concatenate([own_ref[...], gram, across], axis=1)


def parts_kernel(modes_ref, parts_ref):
    def rows(i, carry):
        for j in range(4):
            r = i * 4 + j
            pieces = [
                modes_ref[pl.ds(r * SPAN + q * 8 + s, 8, stride=8), :] for s in range(8) for q in range(0, STEPS, 8)
            ]
            parts_ref[r] = jnp.concatenate(split(jnp.concatenate(pieces, axis=0)), axis=1)
        return carry

    lax.fori_loop(0, ROWS // 4, rows, 0)


def inverse_factors(sums):
    row, lane = iota((8, LANES), 0), iota((8, LANES), 1)
    start = lane // (2 * M) * (2 * M)
    tiles = [
        jnp.where((lane // M) % 2 == 0, sums[8 * t : 8 * t + 8], (lane % M == row + 8 * t).astype(F32))
        for t in range(M // 8)
    ]
    for t in range(M // 8):
        lanes = [start + (8 * t + i) for i in range(8)]
        below = range(t + 1, M // 8)
        columns = [[jnp.take_along_axis(tiles[u], lanes[i], axis=1) for u in below] for i in range(8)]
        rows = [jnp.broadcast_to(tiles[t][i : i + 1], (8, LANES)) for i in range(8)]
        corner = {(i, j): jnp.take_along_axis(rows[i], lanes[j], axis=1) for i in range(8) for j in range(i, 8)}
        inverse, factor = [], {}
        for i in range(8):
            inverse.append(1.0 / corner[i, i])
            for j in range(i + 1, 8):
                factor[j, i] = corner[i, j] * inverse[i]
            for j in range(i + 1, 8):
                for m in range(j, 8):
                    corner[j, m] = corner[j, m] - factor[j, i] * corner[i, m]
        for i in range(8):
            for j in range(i):
                rows[i] = rows[i] - factor[i, j] * rows[j]
                columns[i] = [c - factor[i, j] * p for c, p in zip(columns[i], columns[j])]
        scaled = [rows[i] * inverse[i] for i in range(8)]
        for u in below:
            for i in range(8):
                tiles[u] = tiles[u] - columns[i][u - t - 1] * scaled[i]
        done = rows[0] / jnp.sqrt(corner[0, 0])
        for i in range(1, 8):
            done = jnp.where(row == i, rows[i] / jnp.sqrt(corner[i, i]), done)
        tiles[t] = done
    return jnp.concatenate(tiles, axis=0)


def finish_kernel(sums_ref, parts_ref, modes_ref, proj_ref, corr_ref, held_ref, small_ref, sem):
    sums = sums_ref[...]
    inverse = inverse_factors(sums)
    own, following = inverse[:, M : 2 * M], inverse[:, 3 * M : 4 * M]
    group = iota((M, LANES), 1) // M
    wide = jnp.concatenate([own * math.sqrt(NX * NY)] * GROUPS, axis=1)
    wide = jnp.concatenate([jnp.where(group == g, wide, 0.0) for g in range(GROUPS)], axis=0)
    high, low = split(wide)
    stack = jnp.concatenate([high, high], axis=1)
    stack = jnp.concatenate([stack, jnp.concatenate([low, jnp.zeros_like(low)], axis=1)], axis=0)

    copies = []

    def send(source, target):
        copies.append(pltpu.make_async_copy(source, target, sem.at[len(copies)]))
        copies[-1].start()

    for half in range(2):
        rows = slice(8 * half, 8 * half + 8)
        for r in range(8 * half, 8 * half + 8):
            both = lax.dot_general(stack, parts_ref[r], (((1,), (1,)), ((), ())), preferred_element_type=F32)
            result = both[0:LANES] + both[LANES:]
            for g in range(GROUPS):
                held_ref[:, r, g * SPAN : (g + 1) * SPAN] = result[M * g : M * g + M]
        send(held_ref.at[:, rows], modes_ref.at[:, rows])

    exact = functools.partial(jnp.dot, precision=lax.Precision.HIGHEST, preferred_element_type=F32)
    image, across = sums[:, M : 2 * M], sums[:, 3 * M : 4 * M]
    small_ref[0] = exact(exact(own, image), own.T)
    has_next = lax.axis_index("slab") < lax.axis_size("slab") - 1
    small_ref[1] = jnp.where(has_next, exact(exact(own, across.T), following.T), 0.0)
    send(small_ref.at[0], proj_ref)
    send(small_ref.at[1], corr_ref)
    for copy in copies:
        copy.wait()


def add_over_strips(v):
    def others(x, *masks):
        return [lax.ppermute(x, "xs", [(i, i ^ mask) for i in range(64)]) for mask in masks]

    v = v + others(v, 1)[0]
    for unit in (2, 8):
        one, two, three = others(v, unit, 2 * unit, 3 * unit)
        v = (v + one) + (two + three)
    return v + others(v, 7 * 8)[0]


def local(perturbation, seeds):
    strips = NX // ROWS
    pert = perturbation[0]
    inner = lax.ppermute(pert, "xs", [(i, i ^ 1) for i in range(strips)])
    outer = lax.ppermute(pert, "xs", [(i, i - 1 if i % 2 == 0 else i + 1) for i in range(1, strips - 1)])
    vmem = pl.BlockSpec(memory_space=pltpu.VMEM)
    params = pltpu.CompilerParams(vmem_limit_bytes=28 * 2**20)
    field_shape = (STEPS, 8, LANES)
    middle, *tables = pl.pallas_call(
        prepare_kernel,
        name="prepare",
        out_shape=(
            jax.ShapeDtypeStruct((SENT, NY), jnp.int32),
            jax.ShapeDtypeStruct(field_shape, F32),
            jax.ShapeDtypeStruct((EXT, LANES), F32),
            jax.ShapeDtypeStruct((8, LANES), F32),
            jax.ShapeDtypeStruct((ROWS, *field_shape), F32),
            jax.ShapeDtypeStruct((ROWS, *field_shape), F32),
        ),
        in_specs=[pl.BlockSpec(memory_space=pltpu.HBM)] * 2,
        out_specs=(vmem,) * 6,
        scratch_shapes=[
            pltpu.VMEM((ROWS, NY), jnp.int32),
            pltpu.VMEM((2, M), jnp.int32),
            pltpu.VMEM((SPAN, LANES), F32),
            pltpu.SemaphoreType.DMA((2,)),
        ],
        compiler_params=pltpu.CompilerParams(vmem_limit_bytes=12 * 2**20),
        cost_estimate=pl.CostEstimate(flops=2**26, bytes_accessed=2**22, transcendentals=2**14),
    )(pert, seeds[0].T)
    strip = pl.pallas_call(
        assemble_kernel,
        name="assemble",
        out_shape=jax.ShapeDtypeStruct((SENT, NY), jnp.int32),
        in_specs=[vmem, vmem, vmem],
        out_specs=vmem,
        compiler_params=pltpu.CompilerParams(vmem_limit_bytes=4 * 2**20),
    )(inner, outer, middle)
    following = lax.ppermute(strip, "slab", [((i + 1) % 4, i) for i in range(4)])

    trial = pltpu.VMEM((EXT, *field_shape), F32)
    edges = pltpu.VMEM((2 * HALO, *field_shape), F32)
    turned = pltpu.VMEM((SPAN, LANES), F32)
    cost = pl.CostEstimate(flops=2**30, bytes_accessed=2**23, transcendentals=0)
    field, own = pl.pallas_call(
        own_kernel,
        name="own_trial",
        out_shape=(jax.ShapeDtypeStruct((ROWS * SPAN, LANES), F32), jax.ShapeDtypeStruct((M, 2 * M), F32)),
        in_specs=[vmem] * 7,
        out_specs=(vmem, vmem),
        scratch_shapes=[edges, edges, turned, trial, trial],
        compiler_params=params,
        cost_estimate=cost,
    )(inner, outer, *tables)
    sums = pl.pallas_call(
        next_kernel,
        name="next_trial",
        out_shape=jax.ShapeDtypeStruct((M, 4 * M), F32),
        in_specs=[vmem, vmem, vmem],
        out_specs=vmem,
        scratch_shapes=[trial, turned, trial, trial],
        compiler_params=params,
        cost_estimate=cost,
    )(following, field, own)
    parts = pl.pallas_call(
        parts_kernel,
        name="parts",
        out_shape=jax.ShapeDtypeStruct((ROWS, SPAN, 2 * LANES), BF16),
        in_specs=[vmem],
        out_specs=vmem,
        compiler_params=pltpu.CompilerParams(vmem_limit_bytes=12 * 2**20),
        cost_estimate=pl.CostEstimate(flops=2**20, bytes_accessed=2**22, transcendentals=0),
    )(field)
    sums = add_over_strips(sums)
    modes, projected, correlations = pl.pallas_call(
        finish_kernel,
        name="finish",
        out_shape=(
            jax.ShapeDtypeStruct((M, ROWS, NY), F32),
            jax.ShapeDtypeStruct((M, M), F32),
            jax.ShapeDtypeStruct((M, M), F32),
        ),
        in_specs=[vmem, vmem],
        out_specs=(pl.BlockSpec(memory_space=pl.ANY),) * 3,
        scratch_shapes=[
            pltpu.VMEM((M, ROWS, NY), F32),
            pltpu.VMEM((2, M, M), F32),
            pltpu.SemaphoreType.DMA((4,)),
        ],
        compiler_params=params,
        cost_estimate=pl.CostEstimate(flops=2**28, bytes_accessed=2**23, transcendentals=0),
    )(sums, parts)
    return modes[None], projected[None], correlations[None]


def solution(mesh):
    return jax.shard_map(
        local,
        mesh=mesh,
        in_specs=(P("slab", "xs", None), P("slab", None, None)),
        out_specs=(P("slab", None, "xs", None), P("slab", None, None), P("slab", None, None)),
        check_vma=False,
    )
```

```python
import functools
import math

import jax
import jax.numpy as jnp
from jax import lax
from jax.experimental import pallas as pl
from jax.experimental.pallas import tpu as pltpu
from jax.sharding import PartitionSpec as P

NX = 1024
NY = 1024
M = 32
ROWS = 16
HALO = 4
EXT = ROWS + 2 * HALO
LANES = 128
GROUPS = LANES // M
SPAN = NY // GROUPS
STEPS = SPAN // 8
SENT = EXT
F32 = jnp.float32
BF16 = jnp.bfloat16


def split(x):
    high = x.astype(BF16)
    return high, (x - high.astype(F32)).astype(BF16)


def iota(shape, axis):
    return lax.broadcasted_iota(jnp.int32, shape, axis)


def sine_tables(k, first, second):
    unit = math.pi / (NX + 1)
    base = column_base().astype(F32)
    scale = 2.0 / math.sqrt((NX + 1) * (NY + 1))
    angle = unit * second * (base + 1.0)
    sin_base, cos_base = scale * jnp.sin(angle), scale * jnp.cos(angle)
    step = unit * second * iota((STEPS, LANES), 0).astype(F32)
    sin_step, cos_step = jnp.sin(step), jnp.cos(step)
    sines = [sin_base * cos_step[q : q + 1] + cos_base * sin_step[q : q + 1] for q in range(STEPS)]
    row = iota((EXT, LANES), 0) + (k * ROWS - HALO)
    along_x = jnp.sin(unit * first * (row.astype(F32) + 1.0))
    along_x = jnp.where((row >= 0) & (row < NX), along_x, 0.0)
    return sines, along_x, 2.0 * jnp.cos(unit * first) + 2.0 * jnp.cos(unit * second)


def column_base():
    return iota((8, LANES), 1) // M * SPAN + iota((8, LANES), 0) * STEPS


def first_rows(k, pert, rows, sines, along_x, shift, turned_ref, write):
    count = pert.shape[0]
    xpos = ((iota((EXT, LANES), 0) + (k * ROWS - HALO)).astype(F32) + 0.5) / NX - 0.5
    x_terms = thirds(10.0 * (9.0 - 4.0 * (xpos * xpos + 0.5 * xpos)))
    stacked = [pert[:, g * SPAN : (g + 1) * SPAN] for g in range(GROUPS)]
    stacked = jnp.concatenate(stacked + [jnp.zeros((LANES - GROUPS * count, SPAN), F32)], axis=0)
    turned_ref[...] = jnp.transpose(stacked)

    lane, s = iota((8, LANES), 1), iota((8, LANES), 0)
    term = lane % 4
    base = ((lane - 96) // 4 * SPAN + s * STEPS).astype(F32)
    spread = []
    for q in range(STEPS):
        ypos = (base + (q + 0.5)) / NY - 0.5
        one, two, three = thirds(24.0 * ypos * ypos)
        y_terms = jnp.where(term == 0, one, jnp.where(term == 1, two, jnp.where(term == 2, three, 0.0)))
        extra = jnp.where(lane < 96, 0.0, jnp.where(lane < 112, y_terms, jnp.where(lane < 115, 1.0, 0.0)))
        spread.append(turned_ref[pl.ds(q, 8, stride=STEPS), :] + extra)
    spread = jnp.concatenate(spread, axis=0).astype(BF16)

    line, group = iota((112, LANES), 0), iota((112, LANES), 1) // M
    source = line - count * group
    y_pick = jnp.where((line >= 96) & ((line - 96) // 4 == group), -1.0, 0.0)
    for i, e in rows:
        pick = jnp.where(source == i, -1.0, y_pick)
        parts = [jnp.broadcast_to(part[e : e + 1], (8, LANES)) for part in x_terms]
        x_pick = jnp.where(s == 0, parts[0], jnp.where(s == 1, parts[1], jnp.where(s == 2, parts[2], 0.0)))
        pick = jnp.concatenate([pick, x_pick, jnp.zeros((8, LANES), F32)], axis=0).astype(BF16)
        here = jnp.dot(spread, pick, preferred_element_type=F32)
        sine_row = jnp.broadcast_to(along_x[e : e + 1], (8, LANES))
        for q in range(STEPS):
            w = 0.1 * here[8 * q : 8 * q + 8]
            write(i, e, q, w, (w + shift) * (sine_row * sines[q]))


def thirds(x):
    one = x.astype(BF16).astype(F32)
    two = (x - one).astype(BF16).astype(F32)
    return one, two, (x - one) - two


def prepare_kernel(
    pert_hbm, seeds_hbm, strip_ref, sines_ref, along_ref, shift_ref, w_ref, out_ref, pert_ref, seeds_ref, turned_ref, sem
):
    k = lax.axis_index("xs")
    pert_copy = pltpu.make_async_copy(pert_hbm, pert_ref, sem.at[0])
    seeds_copy = pltpu.make_async_copy(seeds_hbm, seeds_ref, sem.at[1])
    pert_copy.start()
    seeds_copy.start()
    seeds_copy.wait()
    indices = jnp.concatenate([seeds_ref[...]] * GROUPS, axis=1)
    first, second = indices[0:1].astype(F32), indices[1:2].astype(F32)
    sines, along_x, shift = sine_tables(k, first, second)
    for q in range(STEPS):
        sines_ref[q] = sines[q]
    along_ref[...] = along_x
    shift_ref[...] = jnp.broadcast_to(shift, (8, LANES))
    strip_ref[SENT - 2 : SENT - 1, 0:LANES] = indices[0:1]
    strip_ref[SENT - 2 : SENT - 1, LANES : 2 * LANES] = indices[1:2]
    pert_copy.wait()
    strip_ref[HALO - 1 : HALO - 1 + ROWS, :] = pert_ref[...]

    def write(i, e, q, w, value):
        w_ref[i, q] = w
        out_ref[i, q] = value

    rows = [(i, i + HALO) for i in range(ROWS)]
    first_rows(k, pert_ref[...].astype(F32), rows, sines, along_x, shift, turned_ref, write)


def halo(inner_ref, outer_ref):
    even = lax.axis_index("xs") % 2 == 0
    before = jnp.where(even, outer_ref[ROWS - HALO :, :], inner_ref[ROWS - HALO :, :])
    after = jnp.where(even, inner_ref[:HALO, :], outer_ref[:HALO, :])
    return before, after


def assemble_kernel(inner_ref, outer_ref, middle_ref, strip_ref):
    before, after = halo(inner_ref, outer_ref)
    strip_ref[...] = middle_ref[...]
    strip_ref[0 : HALO - 1, :] = before[1:]
    strip_ref[HALO - 1 + ROWS : SENT - 2, :] = after[: HALO - 1]


def beyond(row_first, row_last):
    s, lane = iota((8, LANES), 0), iota((8, LANES), 1)
    down = pltpu.roll(row_last, 1, 0)
    left = jnp.where(s == 0, jnp.where(lane < M, 0.0, pltpu.roll(down, M, 1)), down)
    up = pltpu.roll(row_first, 7, 0)
    right = jnp.where(s == 7, jnp.where(lane >= LANES - M, 0.0, pltpu.roll(up, LANES - M, 1)), up)
    return left, right


def strip_row(i, j):
    return j + i * (EXT - 1 - 2 * j)


def whole(ref):
    return lambda i, j, q: ref[strip_row(i, j), q]


def parted(halo_ref, own_ref):
    def get(i, j, q):
        if j < HALO:
            return halo_ref[j + i * (2 * HALO - 1 - 2 * j), q]
        return own_ref[strip_row(i, j) - HALO, q]

    return get


def sweep(k, margin, source, weight, out_ref, hamiltonian=False):
    first, stop, chunk = HALO - margin, EXT // 2, 4

    def half(i, carry):
        ends = {j: beyond(source(i, j, 0), source(i, j, STEPS - 1)) for j in range(first, stop)}
        inside_grid = jnp.where(k == i * (NX // ROWS - 1), 0.0, 1.0)
        for q0 in range(0, STEPS, chunk):
            inside = range(q0, q0 + chunk)
            x = {(j, q): source(i, j, q) for j in range(first - 1, stop + 1) for q in inside}
            for j in range(first, stop):
                x[j, q0 - 1] = source(i, j, q0 - 1) if q0 > 0 else ends[j][0]
                x[j, q0 + chunk] = source(i, j, q0 + chunk) if q0 + chunk < STEPS else ends[j][1]
            for j in range(first, stop):
                for q in inside:
                    near = (x[j, q - 1] + x[j, q + 1]) + (x[j - 1, q] + x[j + 1, q])
                    if hamiltonian:
                        value = (13.0 - weight(i, j, q)) * x[j, q] - near
                    else:
                        value = weight(i, j, q) * x[j, q] + near
                    if j == HALO - 1:
                        value = value * inside_grid
                    out_ref[strip_row(i, j), q] = value
        return carry

    lax.fori_loop(0, 2, half, 0)


def blocks(product):
    return sum(product[M * g : M * g + M, M * g : M * g + M] for g in range(GROUPS))


def dot_cells(a, b):
    return lax.dot_general(a, b, (((0,), (0,)), ((), ())), preferred_element_type=F32)


def own_kernel(
    inner_ref, outer_ref, sines_ref, along_ref, shift_ref, w_ref, first_ref,
    two_ref, sums_ref, halo_w_ref, halo_ref, turned_ref, one_ref,
):
    k = lax.axis_index("xs")

    def write(i, e, q, w, value):
        halo_w_ref[i, q] = w
        halo_ref[i, q] = value

    pert = jnp.concatenate(halo(inner_ref, outer_ref), axis=0).astype(F32)
    rows = [(i, i if i < HALO else i + ROWS) for i in range(2 * HALO)]
    sines = [sines_ref[q] for q in range(STEPS)]
    first_rows(k, pert, rows, sines, along_ref[...], shift_ref[...], turned_ref, write)
    weight = parted(halo_w_ref, w_ref)
    sweep(k, 3, parted(halo_ref, first_ref), weight, two_ref)
    sweep(k, 2, whole(two_ref), weight, one_ref)
    sweep(k, 1, whole(one_ref), weight, two_ref)
    sweep(k, 0, whole(two_ref), weight, one_ref, hamiltonian=True)
    field = two_ref[HALO : HALO + ROWS].reshape(ROWS * SPAN, LANES)
    image = one_ref[HALO : HALO + ROWS].reshape(ROWS * SPAN, LANES)
    high, low = split(field)
    image_high, image_low = split(image)
    main = dot_cells(high, jnp.concatenate([high, low, image_high, image_low], axis=1))
    rest = blocks(dot_cells(low, image_high))
    cross = blocks(main[:, LANES : 2 * LANES])
    gram = blocks(main[:, 0:LANES]) + (cross + cross.T)
    ham = blocks(main[:, 2 * LANES : 3 * LANES]) + (blocks(main[:, 3 * LANES :]) + rest)
    sums_ref[...] = jnp.concatenate([gram, ham], axis=1)


def next_kernel(strip_ref, modes_ref, own_ref, sums_ref, w_ref, turned_ref, one_ref, two_ref):
    k = lax.axis_index("xs")
    first = strip_ref[SENT - 2 : SENT - 1, 0:LANES].astype(F32)
    second = strip_ref[SENT - 2 : SENT - 1, LANES : 2 * LANES].astype(F32)

    def write(i, e, q, w, value):
        w_ref[e, q] = w
        one_ref[e, q] = value

    rows = [(i, i + 1) for i in range(EXT - 2)]
    first_rows(k, strip_ref[...].astype(F32), rows, *sine_tables(k, first, second), turned_ref, write)
    weight = whole(w_ref)
    sweep(k, 2, whole(one_ref), weight, two_ref)
    sweep(k, 1, whole(two_ref), weight, one_ref)
    sweep(k, 0, whole(one_ref), weight, two_ref)
    field = two_ref[HALO : HALO + ROWS].reshape(ROWS * SPAN, LANES)
    high, low = split(field)
    own_high, own_low = split(modes_ref[HALO : HALO + ROWS].reshape(ROWS * SPAN, LANES))
    main = dot_cells(high, jnp.concatenate([high, low, own_high, own_low], axis=1))
    rest = blocks(dot_cells(low, own_high))
    cross = blocks(main[:, LANES : 2 * LANES])
    gram = blocks(main[:, 0:LANES]) + (cross + cross.T)
    across = blocks(main[:, 2 * LANES : 3 * LANES]) + (blocks(main[:, 3 * LANES :]) + rest)
    sums_ref[...] = jnp.concatenate([own_ref[...], gram, across], axis=1)


def parts_kernel(modes_ref, parts_ref):
    def rows(i, carry):
        for j in range(4):
            r = i * 4 + j
            pieces = [
                modes_ref[pl.ds((r + HALO) * SPAN + q * 8 + s, 8, stride=8), :] for s in range(8) for q in range(0, STEPS, 8)
            ]
            parts_ref[r] = jnp.concatenate(split(jnp.concatenate(pieces, axis=0)), axis=1)
        return carry

    lax.fori_loop(0, ROWS // 4, rows, 0)


def inverse_factors(sums):
    row, lane = iota((8, LANES), 0), iota((8, LANES), 1)
    start = lane // (2 * M) * (2 * M)
    tiles = [
        jnp.where((lane // M) % 2 == 0, sums[8 * t : 8 * t + 8], (lane % M == row + 8 * t).astype(F32))
        for t in range(M // 8)
    ]
    for t in range(M // 8):
        lanes = [start + (8 * t + i) for i in range(8)]
        below = range(t + 1, M // 8)
        columns = [[jnp.take_along_axis(tiles[u], lanes[i], axis=1) for u in below] for i in range(8)]
        rows = [jnp.broadcast_to(tiles[t][i : i + 1], (8, LANES)) for i in range(8)]
        corner = {(i, j): jnp.take_along_axis(rows[i], lanes[j], axis=1) for i in range(8) for j in range(i, 8)}
        inverse, factor = [], {}
        for i in range(8):
            inverse.append(1.0 / corner[i, i])
            for j in range(i + 1, 8):
                factor[j, i] = corner[i, j] * inverse[i]
            for j in range(i + 1, 8):
                for m in range(j, 8):
                    corner[j, m] = corner[j, m] - factor[j, i] * corner[i, m]
        for i in range(8):
            for j in range(i):
                rows[i] = rows[i] - factor[i, j] * rows[j]
                columns[i] = [c - factor[i, j] * p for c, p in zip(columns[i], columns[j])]
        scaled = [rows[i] * inverse[i] for i in range(8)]
        for u in below:
            for i in range(8):
                tiles[u] = tiles[u] - columns[i][u - t - 1] * scaled[i]
        done = rows[0] / jnp.sqrt(corner[0, 0])
        for i in range(1, 8):
            done = jnp.where(row == i, rows[i] / jnp.sqrt(corner[i, i]), done)
        tiles[t] = done
    return jnp.concatenate(tiles, axis=0)


def finish_kernel(sums_ref, parts_ref, modes_ref, proj_ref, corr_ref, held_ref, small_ref, sem):
    sums = sums_ref[...]
    inverse = inverse_factors(sums)
    own, following = inverse[:, M : 2 * M], inverse[:, 3 * M : 4 * M]
    group = iota((M, LANES), 1) // M
    wide = jnp.concatenate([own * math.sqrt(NX * NY)] * GROUPS, axis=1)
    wide = jnp.concatenate([jnp.where(group == g, wide, 0.0) for g in range(GROUPS)], axis=0)
    high, low = split(wide)
    stack = jnp.concatenate([high, high], axis=1)
    stack = jnp.concatenate([stack, jnp.concatenate([low, jnp.zeros_like(low)], axis=1)], axis=0)

    copies = []

    def send(source, target):
        copies.append(pltpu.make_async_copy(source, target, sem.at[len(copies)]))
        copies[-1].start()

    for half in range(2):
        rows = slice(8 * half, 8 * half + 8)
        for r in range(8 * half, 8 * half + 8):
            both = lax.dot_general(stack, parts_ref[r], (((1,), (1,)), ((), ())), preferred_element_type=F32)
            result = both[0:LANES] + both[LANES:]
            for g in range(GROUPS):
                held_ref[:, r, g * SPAN : (g + 1) * SPAN] = result[M * g : M * g + M]
        send(held_ref.at[:, rows], modes_ref.at[:, rows])

    exact = functools.partial(jnp.dot, precision=lax.Precision.HIGHEST, preferred_element_type=F32)
    image, across = sums[:, M : 2 * M], sums[:, 3 * M : 4 * M]
    small_ref[0] = exact(exact(own, image), own.T)
    has_next = lax.axis_index("slab") < lax.axis_size("slab") - 1
    small_ref[1] = jnp.where(has_next, exact(exact(own, across.T), following.T), 0.0)
    send(small_ref.at[0], proj_ref)
    send(small_ref.at[1], corr_ref)
    for copy in copies:
        copy.wait()


def add_over_strips(v):
    def others(x, *masks):
        return [lax.ppermute(x, "xs", [(i, i ^ mask) for i in range(64)]) for mask in masks]

    v = v + others(v, 1)[0]
    for unit in (8, 2):
        one, two, three = others(v, unit, 2 * unit, 3 * unit)
        v = (v + one) + (two + three)
    return v + others(v, 7 * 8)[0]


def local(perturbation, seeds):
    strips = NX // ROWS
    pert = perturbation[0]
    inner = lax.ppermute(pert, "xs", [(i, i ^ 1) for i in range(strips)])
    outer = lax.ppermute(pert, "xs", [(i, i - 1 if i % 2 == 0 else i + 1) for i in range(1, strips - 1)])
    vmem = pl.BlockSpec(memory_space=pltpu.VMEM)
    params = pltpu.CompilerParams(vmem_limit_bytes=28 * 2**20)
    field_shape = (STEPS, 8, LANES)
    middle, *tables = pl.pallas_call(
        prepare_kernel,
        name="prepare",
        out_shape=(
            jax.ShapeDtypeStruct((SENT, NY), jnp.int32),
            jax.ShapeDtypeStruct(field_shape, F32),
            jax.ShapeDtypeStruct((EXT, LANES), F32),
            jax.ShapeDtypeStruct((8, LANES), F32),
            jax.ShapeDtypeStruct((ROWS, *field_shape), F32),
            jax.ShapeDtypeStruct((ROWS, *field_shape), F32),
        ),
        in_specs=[pl.BlockSpec(memory_space=pltpu.HBM)] * 2,
        out_specs=(vmem,) * 6,
        scratch_shapes=[
            pltpu.VMEM((ROWS, NY), jnp.int32),
            pltpu.VMEM((2, M), jnp.int32),
            pltpu.VMEM((SPAN, LANES), F32),
            pltpu.SemaphoreType.DMA((2,)),
        ],
        compiler_params=pltpu.CompilerParams(vmem_limit_bytes=12 * 2**20),
        cost_estimate=pl.CostEstimate(flops=2**26, bytes_accessed=2**22, transcendentals=2**14),
    )(pert, seeds[0].T)
    strip = pl.pallas_call(
        assemble_kernel,
        name="assemble",
        out_shape=jax.ShapeDtypeStruct((SENT, NY), jnp.int32),
        in_specs=[vmem, vmem, vmem],
        out_specs=vmem,
        compiler_params=pltpu.CompilerParams(vmem_limit_bytes=4 * 2**20),
    )(inner, outer, middle)
    following = lax.ppermute(strip, "slab", [((i + 1) % 4, i) for i in range(4)])

    trial = pltpu.VMEM((EXT, *field_shape), F32)
    edges = pltpu.VMEM((2 * HALO, *field_shape), F32)
    turned = pltpu.VMEM((SPAN, LANES), F32)
    cost = pl.CostEstimate(flops=2**30, bytes_accessed=2**23, transcendentals=0)
    field, own = pl.pallas_call(
        own_kernel,
        name="own_trial",
        out_shape=(jax.ShapeDtypeStruct((EXT, *field_shape), F32), jax.ShapeDtypeStruct((M, 2 * M), F32)),
        in_specs=[vmem] * 7,
        out_specs=(vmem, vmem),
        scratch_shapes=[edges, edges, turned, trial],
        compiler_params=params,
        cost_estimate=cost,
    )(inner, outer, *tables)
    sums = pl.pallas_call(
        next_kernel,
        name="next_trial",
        out_shape=jax.ShapeDtypeStruct((M, 4 * M), F32),
        in_specs=[vmem, vmem, vmem],
        out_specs=vmem,
        scratch_shapes=[trial, turned, trial, trial],
        compiler_params=params,
        cost_estimate=cost,
    )(following, field, own)
    parts = pl.pallas_call(
        parts_kernel,
        name="parts",
        out_shape=jax.ShapeDtypeStruct((ROWS, SPAN, 2 * LANES), BF16),
        in_specs=[vmem],
        out_specs=vmem,
        compiler_params=pltpu.CompilerParams(vmem_limit_bytes=12 * 2**20),
        cost_estimate=pl.CostEstimate(flops=2**20, bytes_accessed=2**22, transcendentals=0),
    )(field.reshape(EXT * SPAN, LANES))
    sums = add_over_strips(sums)
    modes, projected, correlations = pl.pallas_call(
        finish_kernel,
        name="finish",
        out_shape=(
            jax.ShapeDtypeStruct((M, ROWS, NY), F32),
            jax.ShapeDtypeStruct((M, M), F32),
            jax.ShapeDtypeStruct((M, M), F32),
        ),
        in_specs=[vmem, vmem],
        out_specs=(pl.BlockSpec(memory_space=pl.ANY),) * 3,
        scratch_shapes=[
            pltpu.VMEM((M, ROWS, NY), F32),
            pltpu.VMEM((2, M, M), F32),
            pltpu.SemaphoreType.DMA((4,)),
        ],
        compiler_params=params,
        cost_estimate=pl.CostEstimate(flops=2**28, bytes_accessed=2**23, transcendentals=0),
    )(sums, parts)
    return modes[None], projected[None], correlations[None]


def solution(mesh):
    return jax.shard_map(
        local,
        mesh=mesh,
        in_specs=(P("slab", "xs", None), P("slab", None, None)),
        out_specs=(P("slab", None, "xs", None), P("slab", None, None), P("slab", None, None)),
        check_vma=False,
    )
```
